128 devices in a mesh: gx: 8 (over y, core), gy: 16 (over x, z).
Axes of the slice: x: 4, y: 4, z: 4, core: 2. Of those that a mesh axis runs over, the one named last changes fastest.
Arguments:
- tokens: bfloat16 [2, 512, 8192], P(None, None, 'gy'), may hold values from -64 to 64
- cache_lengths: int32 [512], P('gy'), may hold values from 128 to 1024, as said below
- key_cache: bfloat16 [512, 1024, 8, 128], P('gy', None, 'gx'), may hold values from -128 to 128
- value_cache: bfloat16 [512, 1024, 8, 128], P('gy', None, 'gx'), may hold values from -6 to 6
- attn_gain: bfloat16 [8192], P('gy'), may hold values from 0.5 to 1.5
- query_weight: bfloat16 [8192, 8192], P('gy', 'gx'), may hold values from -0.0625 to 0.0625
- keyval_weight: bfloat16 [8192, 2048], P('gy', 'gx'), may hold values from -0.0625 to 0.0625
- out_weight: bfloat16 [8192, 8192], P('gx', 'gy'), may hold values from -0.25 to 0.25
- ffn_gain: bfloat16 [8192], P('gy'), may hold values from 0.5 to 1.5
- gate_weight: bfloat16 [8192, 14336], P('gy', 'gx'), may hold values from -0.0625 to 0.0625
- up_weight: bfloat16 [8192, 14336], P('gy', 'gx'), may hold values from -0.0625 to 0.0625
- down_weight: bfloat16 [14336, 8192], P('gx', 'gy'), may hold values from -0.046875 to 0.046875
Outputs:
- layer_out: bfloat16 [2, 512, 8192], P(None, None, 'gy')
The draws below stay inside these ranges and needn't reach their ends.
Inputs may be any that keep to these rules, and one draw needn't show every extreme that they name: `cache_lengths`: some sequence has exactly 1024 cached tokens.
All inputs are finite; a program needn't handle non-finite values.
Results may differ from the reference program's by a relative error of at most 0.0095.
Values may be sent and summed in bfloat16 or wider, within the bound.
No kernel may reach another device: no remote copies, remote signals or barrier semaphores. Data moves between devices by JAX's collectives and lax.ppermute only.
A program may use at most 128 MiB of HBM per device.

```python
import math
import jax
import jax.numpy as jnp
from jax import lax

D = 8192
QH = 64
KVH = 8
HD = 128
FF = 14336
MAXLEN = 1024
GROUP = 8
SEQS = 512
LEN_MIN = 128


def draw_tokens(key, part):
    key = jax.random.fold_in(key, 11)
    keys = jax.random.split(key, 3)
    column = jnp.arange(D, dtype=jnp.float32) / D
    shape = (2, SEQS, D)
    base = jax.random.normal(keys[0], shape, jnp.float32)
    ramp = jnp.sqrt(1.0 + 2.0 * column)
    jitter = jnp.exp(jax.random.uniform(keys[1], (D,), jnp.float32, -0.4, 0.4))
    scales = jnp.exp(jax.random.uniform(keys[2], (2, SEQS, 1), jnp.float32, math.log(0.5), math.log(2.0)))
    return jnp.clip(base * ramp * jitter * scales, -64.0, 64.0).astype(jnp.bfloat16)


def draw_cache_lengths(key, part):
    key = jax.random.fold_in(key, 23)
    draw_key, spot_key = jax.random.split(key)
    drawn = jax.random.randint(draw_key, (SEQS,), LEN_MIN, MAXLEN + 1)
    longest = jax.random.randint(spot_key, (), 0, SEQS)
    return jnp.where(jnp.arange(SEQS) == longest, MAXLEN, drawn).astype(jnp.int32)


def draw_key_cache(key, part):
    key = jax.random.fold_in(key, 37)
    keys = jax.random.split(key, 1)
    shape = (SEQS, MAXLEN, KVH, HD)
    result = jnp.clip(jax.random.normal(keys[0], shape, jnp.float32), -6.0, 6.0)
    return result.astype(jnp.bfloat16)


def levels(rng, dims, pieces, least, top_value):
    level, own = 1.0, jax.random.fold_in(rng, 6)
    for axis_at, parts in pieces:
        draws = jnp.exp(jax.random.uniform(jax.random.fold_in(own, axis_at), (parts,), jnp.float32, least / len(pieces), top_value / len(pieces)))
        level = level * jnp.repeat(draws, dims[axis_at] // parts).reshape([-1 if axis == axis_at else 1 for axis in range(len(dims))])
    return level


def scatter_about(stream_key, dims, spread, reach, pieces=(), held_as=jnp.bfloat16):
    gain = levels(stream_key, dims, pieces, -0.22, 0.18) if pieces else 1.0
    values = jax.random.normal(stream_key, dims, jnp.float32) * spread * gain
    return jnp.minimum(jnp.maximum(values, -reach), reach).astype(held_as)


def setup_inputs(seed: int = 0) -> dict:
    seeds = jax.random.split(jax.random.key(seed), 13)
    tokens = draw_tokens(jax.random.fold_in(seeds[12], 71), 0)
    cache_lengths = draw_cache_lengths(jax.random.fold_in(seeds[12], 71), 0)
    key_cache = draw_key_cache(jax.random.fold_in(seeds[12], 71), 0)
    value_cache = scatter_about(seeds[3], (SEQS, MAXLEN, KVH, HD), 1.0, 6.0, ((0, 16), (2, 8)))
    attn_gain = jnp.clip(1.0 + 0.1 * jax.random.normal(seeds[4], (D,), jnp.float32), 0.5, 1.5).astype(jnp.bfloat16)
    query_weight = scatter_about(seeds[5], (D, QH * HD), D ** -0.5, 0.0625, ((0, 16), (1, 8)))
    keyval_weight = scatter_about(seeds[6], (D, 2 * KVH * HD), D ** -0.5, 0.0625, ((0, 16), (1, 8)))
    out_weight = scatter_about(seeds[7], (QH * HD, D), (QH * HD // 16) ** -0.5, 0.25, ((0, 8), (1, 16)))
    ffn_gain = jnp.clip(1.0 + 0.1 * jax.random.normal(seeds[8], (D,), jnp.float32), 0.5, 1.5).astype(jnp.bfloat16)
    gate_weight = scatter_about(seeds[9], (D, FF), D ** -0.5, 0.0625, ((0, 16), (1, 8)))
    up_weight = scatter_about(seeds[10], (D, FF), D ** -0.5, 0.0625, ((0, 16), (1, 8)))
    down_weight = scatter_about(seeds[11], (FF, D), FF ** -0.5, 0.046875, ((0, 8), (1, 16)))
    return {"tokens": tokens, "cache_lengths": cache_lengths, "key_cache": key_cache, "value_cache": value_cache, "attn_gain": attn_gain, "query_weight": query_weight, "keyval_weight": keyval_weight, "out_weight": out_weight, "ffn_gain": ffn_gain, "gate_weight": gate_weight, "up_weight": up_weight, "down_weight": down_weight}


epsilon = 1e-05
rotary_base = 500000.0

def rotary(values, positions):
    half_dim = HD // 2
    inv_freq = rotary_base ** (-(jnp.arange(half_dim, dtype=jnp.float32) * 2.0 / HD))
    angles = positions[:, None] * inv_freq[None, :]
    cosine = jnp.cos(angles)[:, None, :]
    sine_part = jnp.sin(angles)[:, None, :]
    first_half = values[..., :half_dim]
    second_half = values[..., half_dim:]
    return jnp.concatenate([first_half * cosine - second_half * sine_part, second_half * cosine + first_half * sine_part], axis=-1)

def attend_sequence(operands):
    queries, cached_keys, cached_values, length, extra_keys, extra_values = operands
    scale_factor = 1.0 / math.sqrt(HD)
    grouped = queries.astype(jnp.float32).reshape(KVH, GROUP, HD)
    cached = jnp.einsum('gjd,tgd->gjt', grouped, cached_keys.astype(jnp.float32)) * scale_factor
    valid = jnp.arange(MAXLEN) < length
    cached = jnp.where(valid[None, None, :], cached, -1e+30)
    recent = jnp.einsum('gjd,egd->gje', grouped, extra_keys.astype(jnp.float32)) * scale_factor
    highest = jnp.maximum(lax.optimization_barrier(jnp.max(cached, axis=-1, keepdims=True)), lax.optimization_barrier(jnp.max(recent, axis=-1, keepdims=True)))
    cached_exp = jnp.exp(cached - highest)
    recent_exp = jnp.exp(recent - highest)
    totals = lax.optimization_barrier(jnp.sum(cached_exp, axis=-1, keepdims=True)) + lax.optimization_barrier(jnp.sum(recent_exp, axis=-1, keepdims=True))
    cached_probs = (cached_exp / totals).astype(jnp.bfloat16)
    recent_probs = (recent_exp / totals).astype(jnp.bfloat16)
    mixed = jnp.einsum('gjt,tgd->gjd', cached_probs.astype(jnp.float32), cached_values.astype(jnp.float32))
    mixed = mixed + jnp.einsum('gje,egd->gjd', recent_probs.astype(jnp.float32), extra_values.astype(jnp.float32))
    return mixed.reshape(QH, HD).astype(jnp.bfloat16)

def reference(tokens, cache_lengths, key_cache, value_cache, attn_gain, query_weight, keyval_weight, out_weight, ffn_gain, gate_weight, up_weight, down_weight):
    results = []
    keys_new = []
    values_new = []
    for decode_step in range(2):
        current = tokens[decode_step].astype(jnp.float32)
        attn_ms = lax.optimization_barrier(jnp.mean(current * current, axis=1, keepdims=True))
        normed = (current * lax.rsqrt(attn_ms + epsilon) * attn_gain.astype(jnp.float32)).astype(jnp.bfloat16)
        query_part = jnp.dot(normed, query_weight, preferred_element_type=jnp.float32).reshape(SEQS, QH, HD)
        key_value = jnp.dot(normed, keyval_weight, preferred_element_type=jnp.float32).reshape(SEQS, KVH, 2, HD)
        positions = (cache_lengths + decode_step).astype(jnp.float32)
        queries = rotary(query_part, positions).astype(jnp.bfloat16)
        keys_new.append(rotary(key_value[:, :, 0], positions).astype(jnp.bfloat16))
        values_new.append(key_value[:, :, 1].astype(jnp.bfloat16))
        extra_keys = jnp.stack(keys_new, axis=1)
        extra_values = jnp.stack(values_new, axis=1)
        attended = lax.map(attend_sequence, (queries, key_cache, value_cache, cache_lengths, extra_keys, extra_values))
        attended = attended.reshape(SEQS, QH * HD)
        projected = jnp.dot(attended, out_weight, preferred_element_type=jnp.float32)
        resid = (current + projected).astype(jnp.bfloat16)
        resid_f = resid.astype(jnp.float32)
        ffn_ms = lax.optimization_barrier(jnp.mean(resid_f * resid_f, axis=1, keepdims=True))
        ffn_in = (resid_f * lax.rsqrt(ffn_ms + epsilon) * ffn_gain.astype(jnp.float32)).astype(jnp.bfloat16)
        gate_sum = jnp.dot(ffn_in, gate_weight, preferred_element_type=jnp.float32)
        up_sum = jnp.dot(ffn_in, up_weight, preferred_element_type=jnp.float32)
        activated = (jax.nn.silu(gate_sum) * up_sum).astype(jnp.bfloat16)
        down_sum = jnp.dot(activated, down_weight, preferred_element_type=jnp.float32)
        results.append((resid_f + down_sum).astype(jnp.bfloat16))
    return jnp.stack(results)
```

```python
import math

import jax
import jax.numpy as jnp
from jax import lax
from jax.sharding import PartitionSpec as P

D = 8192
HD = 128
GROUP = 8
bf16 = jnp.bfloat16
f32 = jnp.float32

epsilon = 1e-05
rotary_base = 500000.0


def rotary(values, positions):
    half_dim = HD // 2
    inv_freq = rotary_base ** (-(jnp.arange(half_dim, dtype=f32) * 2.0 / HD))
    angles = positions[:, None] * inv_freq[None, :]
    cosine = jnp.cos(angles)[:, None, :]
    sine_part = jnp.sin(angles)[:, None, :]
    first_half = values[..., :half_dim]
    second_half = values[..., half_dim:]
    return jnp.concatenate(
        [
            first_half * cosine - second_half * sine_part,
            second_half * cosine + first_half * sine_part,
        ],
        axis=-1,
    )


def swap_x(value, r):
    return lax.ppermute(value, "gy", [(j, j ^ (r * 4)) for j in range(16)])


def swap_z(value, r):
    return lax.ppermute(value, "gy", [(j, j ^ r) for j in range(16)])


def swap_y(value, r):
    return lax.ppermute(value, "gx", [(g, g ^ (r * 2)) for g in range(8)])


def swap_core(value):
    return lax.ppermute(value, "gx", [(g, g ^ 1) for g in range(8)])


def scatter_sum(value, swap):
    rows = value.shape[0] // 4
    got = [swap(value[r * rows : (r + 1) * rows], r) for r in (1, 2, 3)]
    total = value[:rows].astype(f32)
    for item in got:
        total = total + item.astype(f32)
    return total


def gather_rows(value, swap):
    return jnp.concatenate([value] + [swap(value, r) for r in (1, 2, 3)], axis=0)


ORDERS = ((swap_x, swap_z), (swap_z, swap_x))


def scatter_gy(value, flow):
    first, second = ORDERS[flow]
    return scatter_sum(scatter_sum(value, first).astype(bf16), second)


def gather_gy(value, flow):
    first, second = ORDERS[flow]
    return gather_rows(gather_rows(value, second), first)


def scatter_gx(value, core, row):
    half = value.shape[0] // 2
    kept = lax.dynamic_slice_in_dim(value, core * half, half, 0)
    sent = lax.dynamic_slice_in_dim(value, (1 - core) * half, half, 0)
    both = (kept.astype(f32) + swap_core(sent).astype(f32)).astype(bf16)
    rows = half // 4
    total = lax.dynamic_slice_in_dim(both, row * rows, rows, 0).astype(f32)
    for r in (1, 2, 3):
        part = lax.dynamic_slice_in_dim(both, (row ^ r) * rows, rows, 0)
        total = total + swap_y(part, r).astype(f32)
    return total


def gather_gx(value):
    four = gather_rows(value, swap_y)
    return jnp.concatenate([four, swap_core(four)], axis=0)


def attend(queries, cached_keys, cached_values, lengths, extra_keys, extra_values):
    scale_factor = 1.0 / math.sqrt(HD)
    cached = (
        jnp.einsum("sqd,std->sqt", queries, cached_keys, preferred_element_type=f32)
        * scale_factor
    )
    valid = jnp.arange(cached_keys.shape[1])[None, :] < lengths[:, None]
    cached = jnp.where(valid[:, None, :], cached, -1e30)
    recent = (
        jnp.sum(
            queries.astype(f32)[:, :, None, :] * extra_keys.astype(f32)[:, None, :, :], axis=-1
        )
        * scale_factor
    )
    step_of = jnp.arange(2 * GROUP) // GROUP
    seen = jnp.arange(2)[None, :] <= step_of[:, None]
    recent = jnp.where(seen[None], recent, -1e30)
    highest = jnp.maximum(
        jnp.max(cached, axis=-1, keepdims=True), jnp.max(recent, axis=-1, keepdims=True)
    )
    cached_exp = jnp.exp(cached - highest)
    recent_exp = jnp.exp(recent - highest)
    totals = jnp.sum(cached_exp, axis=-1, keepdims=True) + jnp.sum(
        recent_exp, axis=-1, keepdims=True
    )
    cached_probs = (cached_exp / totals).astype(bf16)
    recent_probs = (recent_exp / totals).astype(bf16).astype(f32)
    mixed = jnp.einsum("sqt,std->sqd", cached_probs, cached_values, preferred_element_type=f32)
    for e in range(2):
        mixed = mixed + recent_probs[:, :, e, None] * extra_values[:, e].astype(f32)[:, None, :]
    return mixed.astype(bf16)


def per_device(
    tokens,
    cache_lengths,
    key_cache,
    value_cache,
    attn_gain,
    query_weight,
    keyval_weight,
    out_weight,
    ffn_gain,
    gate_weight,
    up_weight,
    down_weight,
):
    steps, count, width = tokens.shape
    seqs = cache_lengths.shape[0]
    query_cols = query_weight.shape[1]
    hidden = gate_weight.shape[1]
    me = lax.axis_index("gy")
    mine = lax.axis_index("gx")
    row, core = mine // 2, mine % 2

    place = jnp.arange(count)
    block, inner = place // seqs, place % seqs
    away = (block, (block % 4) * 4 + block // 4)
    token_at = [(me ^ away[f]) * seqs + inner for f in range(2)]
    slot = count // 8
    part = place // slot
    row_at = ((part // 4) ^ core) * (4 * slot) + ((part % 4) ^ row) * slot + place % slot
    order_gx = (place[:, None] == row_at[None, :]).astype(bf16)

    def product(a, b):
        return jnp.dot(a, b, preferred_element_type=f32)

    def with_squares(parts, squares):
        extra = jnp.broadcast_to(squares[:, None], (squares.shape[0], 128))
        return jnp.concatenate([p.astype(bf16) for p in parts + [extra]], axis=1)

    currents, packed = [], []
    for f in range(2):
        order = (token_at[f][:, None] == place[None, :]).astype(bf16)
        current = product(order, tokens[f]).astype(bf16)
        currents.append(current)
        wide = current.astype(f32)
        scaled = (wide * attn_gain.astype(f32)).astype(bf16)
        packed.append(
            with_squares(
                [product(scaled, query_weight), product(scaled, keyval_weight)],
                jnp.sum(wide * wide, axis=1),
            )
        )
    queries, keys_new, values_new = [], [], []
    for f in range(2):
        summed = scatter_gy(packed[f], f)
        scale = lax.rsqrt(summed[:, query_cols + 2 * HD :][:, :1] / D + epsilon)
        projected = summed[:, : query_cols + 2 * HD] * scale
        positions = (cache_lengths + f).astype(f32)
        rotated = rotary(
            projected[:, : query_cols + HD].reshape(seqs, -1, HD), positions
        ).astype(bf16)
        queries.append(rotated[:, :GROUP])
        keys_new.append(rotated[:, GROUP])
        values_new.append(projected[:, query_cols + HD :].astype(bf16))
    attended = attend(
        jnp.concatenate(queries, axis=1),
        key_cache[:, :, 0],
        value_cache[:, :, 0],
        cache_lengths,
        jnp.stack(keys_new, axis=1),
        jnp.stack(values_new, axis=1),
    )
    resid_own, packed = [], []
    for f in range(2):
        mixed = attended[:, f * GROUP : (f + 1) * GROUP].reshape(seqs, query_cols)
        partial_out = product(gather_gy(mixed, f), out_weight).astype(bf16)
        own = lax.dynamic_slice_in_dim(currents[f], (core * 4 + row) * slot, slot, 0)
        own = (own.astype(f32) + scatter_gx(partial_out, core, row)).astype(bf16)
        resid_own.append(own)
        resid = product(order_gx, gather_gx(own))
        scaled = (resid * ffn_gain.astype(f32)).astype(bf16)
        packed.append(
            with_squares(
                [product(scaled, gate_weight), product(scaled, up_weight)],
                jnp.sum(resid * resid, axis=1),
            )
        )
    results = []
    for f in range(2):
        summed = scatter_gy(packed[f], f)
        scale = lax.rsqrt(summed[:, 2 * hidden :][:, :1] / D + epsilon)
        gate = summed[:, :hidden] * scale
        up = summed[:, hidden : 2 * hidden] * scale
        activated = (jax.nn.silu(gate) * up).astype(bf16)
        down = product(gather_gy(activated, f), down_weight).astype(bf16)
        own = (resid_own[f].astype(f32) + scatter_gx(down, core, row)).astype(bf16)
        token_of = jnp.sum(
            jnp.where(row_at[:, None] == place[None, :], token_at[f][None, :], 0), axis=1
        )
        order = (place[:, None] == token_of[None, :]).astype(bf16)
        results.append(product(order, gather_gx(own)).astype(bf16))
    return jnp.stack(results)


def solution(mesh):
    in_specs = (
        P(None, None, "gy"),
        P("gy"),
        P("gy", None, "gx", None),
        P("gy", None, "gx", None),
        P("gy"),
        P("gy", "gx"),
        P("gy", "gx"),
        P("gx", "gy"),
        P("gy"),
        P("gy", "gx"),
        P("gy", "gx"),
        P("gx", "gy"),
    )
    out_specs = P(None, None, "gy")
    return jax.shard_map(
        per_device, mesh=mesh, in_specs=in_specs, out_specs=out_specs, check_vma=False
    )
```

```python
import math

import jax
import jax.numpy as jnp
from jax import lax
from jax.sharding import PartitionSpec as P

D = 8192
HD = 128
GROUP = 8
bf16 = jnp.bfloat16
f32 = jnp.float32

epsilon = 1e-05
rotary_base = 500000.0


def rotary(values, positions):
    half_dim = HD // 2
    inv_freq = rotary_base ** (-(jnp.arange(half_dim, dtype=f32) * 2.0 / HD))
    angles = positions[:, None] * inv_freq[None, :]
    cosine = jnp.cos(angles)[:, None, :]
    sine_part = jnp.sin(angles)[:, None, :]
    first_half = values[..., :half_dim]
    second_half = values[..., half_dim:]
    return jnp.concatenate(
        [
            first_half * cosine - second_half * sine_part,
            second_half * cosine + first_half * sine_part,
        ],
        axis=-1,
    )


GY_MASK = {"x1": 4, "x3": 12, "z1": 1, "z3": 3}
GX_MASK = {"y1": 2, "y3": 6, "core": 1}
ORDERS = (
    ("x1", "z1", "x3", "z3"),
    ("z1", "x3", "z3", "x1"),
    ("x3", "z3", "x1", "z1"),
    ("z3", "x1", "z1", "x3"),
)
FLOWS = len(ORDERS)


def swap(value, pairing):
    if pairing in GY_MASK:
        return lax.ppermute(value, "gy", [(j, j ^ GY_MASK[pairing]) for j in range(16)])
    return lax.ppermute(value, "gx", [(g, g ^ GX_MASK[pairing]) for g in range(8)])


def scatter_gy(flows):
    for step in range(4):
        half = flows[0].shape[0] // 2
        got = [swap(v[half:], ORDERS[f][step]) for f, v in enumerate(flows)]
        flows = [v[:half].astype(f32) + g.astype(f32) for v, g in zip(flows, got)]
        if step < 3:
            flows = [v.astype(bf16) for v in flows]
    return flows


def gather_gy(flows):
    for step in reversed(range(4)):
        got = [swap(v, ORDERS[f][step]) for f, v in enumerate(flows)]
        flows = [jnp.concatenate([v, g], axis=0) for v, g in zip(flows, got)]
    return flows


def sum_gx(value, core):
    half = value.shape[0] // 2
    kept = lax.dynamic_slice_in_dim(value, core * half, half, 0)
    sent = lax.dynamic_slice_in_dim(value, (1 - core) * half, half, 0)
    total = kept.astype(f32) + swap(sent, "core").astype(f32)
    quarter = half // 2
    parts = [total[:quarter], total[quarter:]]
    for pairings in (("y1", "y3"), ("y3", "y1")):
        parts = [p.astype(bf16) for p in parts]
        got = [swap(p, pairing) for p, pairing in zip(parts, pairings)]
        parts = [p.astype(f32) + g.astype(f32) for p, g in zip(parts, got)]
    return jnp.concatenate(parts, axis=0)


def join_core(value, core):
    other = swap(value, "core")
    first = core == 0
    return jnp.concatenate(
        [jnp.where(first, value, other), jnp.where(first, other, value)], axis=0
    )


def attend(queries, cached_keys, cached_values, lengths, extra_keys, extra_values):
    scale_factor = 1.0 / math.sqrt(HD)
    cached = (
        jnp.einsum("sqd,std->sqt", queries, cached_keys, preferred_element_type=f32)
        * scale_factor
    )
    valid = jnp.arange(cached_keys.shape[1])[None, :] < lengths[:, None]
    cached = jnp.where(valid[:, None, :], cached, -1e30)
    recent = (
        jnp.sum(
            queries.astype(f32)[:, :, None, :] * extra_keys.astype(f32)[:, None, :, :], axis=-1
        )
        * scale_factor
    )
    step_of = jnp.arange(2 * GROUP) // GROUP
    seen = jnp.arange(2)[None, :] <= step_of[:, None]
    recent = jnp.where(seen[None], recent, -1e30)
    highest = jnp.maximum(
        jnp.max(cached, axis=-1, keepdims=True), jnp.max(recent, axis=-1, keepdims=True)
    )
    cached_exp = jnp.exp(cached - highest)
    recent_exp = jnp.exp(recent - highest)
    totals = jnp.sum(cached_exp, axis=-1, keepdims=True) + jnp.sum(
        recent_exp, axis=-1, keepdims=True
    )
    cached_probs = (cached_exp / totals).astype(bf16)
    recent_probs = (recent_exp / totals).astype(bf16).astype(f32)
    mixed = jnp.einsum("sqt,std->sqd", cached_probs, cached_values, preferred_element_type=f32)
    for e in range(2):
        mixed = mixed + recent_probs[:, :, e, None] * extra_values[:, e].astype(f32)[:, None, :]
    return mixed.astype(bf16)


def per_device(
    tokens,
    cache_lengths,
    key_cache,
    value_cache,
    attn_gain,
    query_weight,
    keyval_weight,
    out_weight,
    ffn_gain,
    gate_weight,
    up_weight,
    down_weight,
):
    steps, count, width = tokens.shape
    seqs = cache_lengths.shape[0]
    query_cols = query_weight.shape[1]
    hidden = gate_weight.shape[1]
    me = lax.axis_index("gy")
    core = lax.axis_index("gx") % 2
    run = seqs // 2
    flow_rows = 16 * run
    place = jnp.arange(flow_rows)
    block, inner = place // run, place % run
    orders = []
    for f in range(FLOWS):
        away = 0
        for bit, pairing in enumerate(ORDERS[f]):
            away = away ^ (((block >> (3 - bit)) & 1) * GY_MASK[pairing])
        token_at = (me ^ away) * seqs + (f % 2) * run + inner
        orders.append((token_at[:, None] == jnp.arange(count)[None, :]).astype(bf16))

    def product(a, b):
        return jnp.dot(a, b, preferred_element_type=f32)

    def with_squares(parts, squares):
        extra = jnp.broadcast_to(squares[:, None], (squares.shape[0], 128))
        return jnp.concatenate([p.astype(bf16) for p in parts + [extra]], axis=1)

    currents, packed = [], []
    for f in range(FLOWS):
        current = product(orders[f], tokens[f // 2]).astype(bf16)
        currents.append(current)
        wide = current.astype(f32)
        scaled = (wide * attn_gain.astype(f32)).astype(bf16)
        packed.append(
            with_squares(
                [product(scaled, query_weight), product(scaled, keyval_weight)],
                jnp.sum(wide * wide, axis=1),
            )
        )
    summed = scatter_gy(packed)
    queries, keys_new, values_new = [], [], []
    for s in range(steps):
        joined = jnp.concatenate(summed[2 * s : 2 * s + 2], axis=0)
        scale = lax.rsqrt(joined[:, query_cols + 2 * HD :][:, :1] / D + epsilon)
        projected = joined[:, : query_cols + 2 * HD] * scale
        positions = (cache_lengths + s).astype(f32)
        rotated = rotary(
            projected[:, : query_cols + HD].reshape(seqs, -1, HD), positions
        ).astype(bf16)
        queries.append(rotated[:, :GROUP])
        keys_new.append(rotated[:, GROUP])
        values_new.append(projected[:, query_cols + HD :].astype(bf16))
    attended = attend(
        jnp.concatenate(queries, axis=1),
        key_cache[:, :, 0],
        value_cache[:, :, 0],
        cache_lengths,
        jnp.stack(keys_new, axis=1),
        jnp.stack(values_new, axis=1),
    )
    mixed = [
        attended[(f % 2) * run :][:run, (f // 2) * GROUP :][:, :GROUP].reshape(run, query_cols)
        for f in range(FLOWS)
    ]
    gathered = gather_gy(mixed)
    partial_out = jnp.concatenate([product(g, out_weight).astype(bf16) for g in gathered], axis=0)
    current = jnp.concatenate(currents, axis=0)
    own = lax.dynamic_slice_in_dim(current, core * count, count, 0)
    resid_own = (own.astype(f32) + sum_gx(partial_out, core)).astype(bf16)
    resid = join_core(resid_own, core).astype(f32)
    scaled = (resid * ffn_gain.astype(f32)).astype(bf16)
    squares = jnp.sum(resid * resid, axis=1)
    packed = []
    for f in range(FLOWS):
        rows = slice(f * flow_rows, (f + 1) * flow_rows)
        packed.append(
            with_squares(
                [product(scaled[rows], gate_weight), product(scaled[rows], up_weight)],
                squares[rows],
            )
        )
    activated = []
    for total in scatter_gy(packed):
        scale = lax.rsqrt(total[:, 2 * hidden :][:, :1] / D + epsilon)
        gate = total[:, :hidden] * scale
        up = total[:, hidden : 2 * hidden] * scale
        activated.append((jax.nn.silu(gate) * up).astype(bf16))
    gathered = gather_gy(activated)
    down = jnp.concatenate([product(g, down_weight).astype(bf16) for g in gathered], axis=0)
    own = (resid_own.astype(f32) + sum_gx(down, core)).astype(bf16)
    final = join_core(own, core)
    results = []
    for s in range(steps):
        order = jnp.concatenate(orders[2 * s : 2 * s + 2], axis=0)
        rows = final[s * count : (s + 1) * count]
        results.append(
            lax.dot_general(
                order, rows, (((0,), (0,)), ((), ())), preferred_element_type=f32
            ).astype(bf16)
        )
    return jnp.stack(results)


def solution(mesh):
    in_specs = (
        P(None, None, "gy"),
        P("gy"),
        P("gy", None, "gx", None),
        P("gy", None, "gx", None),
        P("gy"),
        P("gy", "gx"),
        P("gy", "gx"),
        P("gx", "gy"),
        P("gy"),
        P("gy", "gx"),
        P("gy", "gx"),
        P("gx", "gy"),
    )
    out_specs = P(None, None, "gy")
    return jax.shard_map(
        per_device, mesh=mesh, in_specs=in_specs, out_specs=out_specs, check_vma=False
    )
```

```python
import math

import jax
import jax.numpy as jnp
from jax import lax
from jax.experimental import pallas as pl
from jax.experimental.pallas import tpu as pltpu
from jax.sharding import PartitionSpec as P

D = 8192
HD = 128
GROUP = 8
bf16 = jnp.bfloat16
f32 = jnp.float32

epsilon = 1e-05
rotary_base = 500000.0


def rotary(values, positions):
    half_dim = HD // 2
    inv_freq = rotary_base ** (-(jnp.arange(half_dim, dtype=f32) * 2.0 / HD))
    angles = positions[:, None] * inv_freq[None, :]
    cosine = jnp.cos(angles)[:, None, :]
    sine_part = jnp.sin(angles)[:, None, :]
    first_half = values[..., :half_dim]
    second_half = values[..., half_dim:]
    return jnp.concatenate(
        [
            first_half * cosine - second_half * sine_part,
            second_half * cosine + first_half * sine_part,
        ],
        axis=-1,
    )


GY_MASK = {"x1": 4, "x3": 12, "z1": 1, "z3": 3}
GX_MASK = {"y1": 2, "y3": 6, "core": 1}
ORDERS = (
    (("x1", "z1", "x3", "z3"), ("z3", "x3", "z1", "x1")),
    (("x3", "z3", "x1", "z1"), ("z1", "x1", "z3", "x3")),
)


def swap(value, pairing):
    if pairing in GY_MASK:
        return lax.ppermute(value, "gy", [(j, j ^ GY_MASK[pairing]) for j in range(16)])
    return lax.ppermute(value, "gx", [(g, g ^ GX_MASK[pairing]) for g in range(8)])


def add(a, b):
    return a.astype(f32) + b.astype(f32)


def scatter_gy(kept, sent, orders, both):
    got = [swap(v, orders[f][0]) for f, v in enumerate(sent)]
    flows = [add(v, g).astype(bf16) for v, g in zip(kept, got)]
    for step in (1, 2):
        half = flows[0].shape[0] // 2
        got = [swap(v[half:], orders[f][step]) for f, v in enumerate(flows)]
        flows = [add(v[:half], g).astype(bf16) for v, g in zip(flows, got)]
    half = flows[0].shape[0] // 2
    if both:
        got = [swap(v, orders[f][3]) for f, v in enumerate(flows)]
        got = [jnp.concatenate([g[half:], g[:half]], axis=0) for g in got]
        return [add(v, g) for v, g in zip(flows, got)]
    got = [swap(v[half:], orders[f][3]) for f, v in enumerate(flows)]
    return [add(v[:half], g) for v, g in zip(flows, got)]


def gather_gy(flows, orders, have):
    for step in reversed(range(4 - have)):
        got = [swap(v, orders[f][step]) for f, v in enumerate(flows)]
        flows = [jnp.concatenate([v, g], axis=0) for v, g in zip(flows, got)]
    return flows


def sum_gx(value, core):
    half = value.shape[0] // 2
    kept = lax.dynamic_slice_in_dim(value, core * half, half, 0)
    sent = lax.dynamic_slice_in_dim(value, (1 - core) * half, half, 0)
    total = kept.astype(f32) + swap(sent, "core").astype(f32)
    quarter = half // 2
    parts = [total[:quarter], total[quarter:]]
    for pairings in (("y1", "y3"), ("y3", "y1")):
        parts = [p.astype(bf16) for p in parts]
        got = [swap(p, pairing) for p, pairing in zip(parts, pairings)]
        parts = [p.astype(f32) + g.astype(f32) for p, g in zip(parts, got)]
    return jnp.concatenate(parts, axis=0)


def join_core(value, core):
    other = swap(value, "core")
    first = core == 0
    return jnp.concatenate(
        [jnp.where(first, value, other), jnp.where(first, other, value)], axis=0
    )


def project_kernel(at_ref, tokens_ref, gain_ref, query_ref, keyval_ref, *outs):
    kept, sent, own = outs[:4], outs[4:8], outs[8:]
    steps, count, _ = tokens_ref.shape
    rows = count // 2
    half = rows // 2
    run = rows // 16
    query_cols = query_ref.shape[1]
    cols = query_cols + keyval_ref.shape[1]
    me, core = at_ref[0], at_ref[1]
    place = lax.broadcasted_iota(jnp.int32, (rows, 128), 0)
    lane = lax.broadcasted_iota(jnp.int32, (rows, 128), 1)
    block, inner = place // run, place % run
    gain = gain_ref[...].astype(f32)
    for part in range(2):
        for s in range(steps):
            f = part * steps + s
            away = jnp.zeros_like(block)
            for bit, pairing in enumerate(ORDERS[part][s]):
                away = away ^ (((block >> (3 - bit)) & 1) * GY_MASK[pairing])
            token_at = (me ^ away) * (2 * run) + part * run + inner
            order = jnp.concatenate(
                [
                    jnp.where(token_at == lane + first, 1.0, 0.0).astype(bf16)
                    for first in range(0, count, 128)
                ],
                axis=1,
            )
            current = jnp.dot(order, tokens_ref[s], preferred_element_type=f32)

            @pl.when(core == s)
            def _(current=current, part=part):
                own[part][...] = current.astype(bf16)

            squares = jnp.sum(current * current, axis=1, keepdims=True)
            squares = jnp.broadcast_to(squares, (rows, 128)).astype(bf16)
            scaled = (current * gain).astype(bf16)
            query = jnp.dot(scaled, query_ref[...], preferred_element_type=f32).astype(bf16)
            keyval = jnp.dot(scaled, keyval_ref[...], preferred_element_type=f32).astype(bf16)
            for ref, at in ((kept[f], slice(0, half)), (sent[f], slice(half, rows))):
                ref[:, :query_cols] = query[at]
                ref[:, query_cols:cols] = keyval[at]
                ref[:, cols:] = squares[at]


def project(at, tokens, gain, query_weight, keyval_weight):
    steps, count, width = tokens.shape
    cols = query_weight.shape[1] + keyval_weight.shape[1] + 128
    rows = count // 2
    vmem = pl.BlockSpec(memory_space=pltpu.VMEM)
    flow = jax.ShapeDtypeStruct((rows // 2, cols), bf16)
    own = jax.ShapeDtypeStruct((rows, width), bf16)
    outs = pl.pallas_call(
        project_kernel,
        out_shape=[flow] * 8 + [own] * 2,
        in_specs=[pl.BlockSpec(memory_space=pltpu.SMEM)] + [vmem] * 4,
        out_specs=[vmem] * 10,
        compiler_params=pltpu.CompilerParams(vmem_limit_bytes=32 * 2**20),
        cost_estimate=pl.CostEstimate(
            flops=2 * steps * count * width * (count + cols),
            bytes_accessed=8 * 2**20,
            transcendentals=0,
        ),
    )(at, tokens, gain.reshape(1, width), query_weight, keyval_weight)
    return outs[:4], outs[4:8], outs[8:]


def attend(queries, cached_keys, cached_values, lengths, extra_keys, extra_values):
    scale_factor = 1.0 / math.sqrt(HD)
    cached = (
        jnp.einsum("sqd,std->sqt", queries, cached_keys, preferred_element_type=f32)
        * scale_factor
    )
    valid = jnp.arange(cached_keys.shape[1])[None, :] < lengths[:, None]
    cached = jnp.where(valid[:, None, :], cached, -1e30)
    recent = (
        jnp.sum(
            queries.astype(f32)[:, :, None, :] * extra_keys.astype(f32)[:, None, :, :], axis=-1
        )
        * scale_factor
    )
    step_of = jnp.arange(2 * GROUP) // GROUP
    seen = jnp.arange(2)[None, :] <= step_of[:, None]
    recent = jnp.where(seen[None], recent, -1e30)
    highest = jnp.maximum(
        jnp.max(cached, axis=-1, keepdims=True), jnp.max(recent, axis=-1, keepdims=True)
    )
    cached_exp = jnp.exp(cached - highest)
    recent_exp = jnp.exp(recent - highest)
    totals = jnp.sum(cached_exp, axis=-1, keepdims=True) + jnp.sum(
        recent_exp, axis=-1, keepdims=True
    )
    cached_probs = (cached_exp / totals).astype(bf16)
    recent_probs = (recent_exp / totals).astype(bf16).astype(f32)
    mixed = jnp.einsum("sqt,std->sqd", cached_probs, cached_values, preferred_element_type=f32)
    for e in range(2):
        mixed = mixed + recent_probs[:, :, e, None] * extra_values[:, e].astype(f32)[:, None, :]
    return mixed.astype(bf16)


def per_device(
    tokens,
    cache_lengths,
    key_cache,
    value_cache,
    attn_gain,
    query_weight,
    keyval_weight,
    out_weight,
    ffn_gain,
    gate_weight,
    up_weight,
    down_weight,
):
    steps, count, width = tokens.shape
    seqs = cache_lengths.shape[0]
    query_cols = query_weight.shape[1]
    hidden = gate_weight.shape[1]
    me = lax.axis_index("gy")
    core = lax.axis_index("gx") % 2
    run = seqs // 2
    flow_rows = 16 * run
    place = jnp.arange(flow_rows)
    block, inner = place // run, place % run

    def product(a, b):
        return jnp.dot(a, b, preferred_element_type=f32)

    def with_squares(parts, squares):
        extra = jnp.broadcast_to(squares[:, None], (squares.shape[0], 128))
        return jnp.concatenate([p.astype(bf16) for p in parts + [extra]], axis=1)

    def order_of(part, s):
        away = 0
        for bit, pairing in enumerate(ORDERS[part][s]):
            away = away ^ (((block >> (3 - bit)) & 1) * GY_MASK[pairing])
        token_at = (me ^ away) * seqs + part * run + inner
        return (token_at[:, None] == jnp.arange(count)[None, :]).astype(bf16)

    def attention(part, summed):
        own = slice(part * run, (part + 1) * run)
        lengths = cache_lengths[own]
        queries, keys_new, values_new = [], [], []
        for s in range(steps):
            scale = lax.rsqrt(summed[s][:, query_cols + 2 * HD :][:, :1] / D + epsilon)
            projected = summed[s][:, : query_cols + 2 * HD] * scale
            rotated = rotary(
                projected[:, : query_cols + HD].reshape(run, -1, HD), (lengths + s).astype(f32)
            ).astype(bf16)
            queries.append(rotated[:, :GROUP])
            keys_new.append(rotated[:, GROUP])
            values_new.append(projected[:, query_cols + HD :].astype(bf16))
        attended = attend(
            jnp.concatenate(queries, axis=1),
            key_cache[own, :, 0],
            value_cache[own, :, 0],
            lengths,
            jnp.stack(keys_new, axis=1),
            jnp.stack(values_new, axis=1),
        )
        return [
            attended[:, s * GROUP : (s + 1) * GROUP].reshape(run, query_cols)
            for s in range(steps)
        ]

    def summed_product(part, flows, weight, have):
        gathered = gather_gy(flows, ORDERS[part], have)
        parts = jnp.concatenate([product(g, weight).astype(bf16) for g in gathered], axis=0)
        return sum_gx(parts, core)

    def feed(part, resid_own):
        resid = join_core(resid_own, core).astype(f32)
        scaled = (resid * ffn_gain.astype(f32)).astype(bf16)
        squares = jnp.sum(resid * resid, axis=1)
        packed = []
        for f in range(steps):
            rows = slice(f * flow_rows, (f + 1) * flow_rows)
            packed.append(
                with_squares(
                    [product(scaled[rows], gate_weight), product(scaled[rows], up_weight)],
                    squares[rows],
                )
            )
        return packed

    def activate(total):
        scale = lax.rsqrt(total[:, 2 * hidden :][:, :1] / D + epsilon)
        gate = total[:, :hidden] * scale
        up = total[:, hidden : 2 * hidden] * scale
        return (jax.nn.silu(gate) * up).astype(bf16)

    halves = range(2)
    at = jnp.stack([me, core]).astype(jnp.int32)
    kept, sent, current = project(at, tokens, attn_gain, query_weight, keyval_weight)
    summed = [
        scatter_gy(kept[2 * p : 2 * p + 2], sent[2 * p : 2 * p + 2], ORDERS[p], False)
        for p in halves
    ]
    mixed = [attention(p, summed[p]) for p in halves]
    outs = [summed_product(p, mixed[p], out_weight, 0) for p in halves]
    resid_own = [(current[p].astype(f32) + outs[p]).astype(bf16) for p in halves]
    packed = [feed(p, resid_own[p]) for p in halves]
    half = flow_rows // 2
    totals = [
        scatter_gy([v[:half] for v in packed[p]], [v[half:] for v in packed[p]], ORDERS[p], True)
        for p in halves
    ]
    activated = [[activate(t) for t in totals[p]] for p in halves]
    downs = [summed_product(p, activated[p], down_weight, 1) for p in halves]
    finals = [
        join_core((resid_own[p].astype(f32) + downs[p]).astype(bf16), core) for p in halves
    ]
    results = []
    for s in range(steps):
        order = jnp.concatenate([order_of(p, s) for p in halves], axis=0)
        rows = jnp.concatenate(
            [finals[p][s * flow_rows : (s + 1) * flow_rows] for p in halves], axis=0
        )
        results.append(
            lax.dot_general(
                order, rows, (((0,), (0,)), ((), ())), preferred_element_type=f32
            ).astype(bf16)
        )
    return jnp.stack(results)


def solution(mesh):
    in_specs = (
        P(None, None, "gy"),
        P("gy"),
        P("gy", None, "gx", None),
        P("gy", None, "gx", None),
        P("gy"),
        P("gy", "gx"),
        P("gy", "gx"),
        P("gx", "gy"),
        P("gy"),
        P("gy", "gx"),
        P("gy", "gx"),
        P("gx", "gy"),
    )
    out_specs = P(None, None, "gy")
    return jax.shard_map(
        per_device, mesh=mesh, in_specs=in_specs, out_specs=out_specs, check_vma=False
    )
```

```python
import math

import jax
import jax.numpy as jnp
from jax import lax
from jax.experimental import pallas as pl
from jax.experimental.pallas import tpu as pltpu
from jax.sharding import PartitionSpec as P

D = 8192
HD = 128
GROUP = 8
bf16 = jnp.bfloat16
f32 = jnp.float32

epsilon = 1e-05
rotary_base = 500000.0


def rotary(values, positions):
    half_dim = HD // 2
    inv_freq = rotary_base ** (-(jnp.arange(half_dim, dtype=f32) * 2.0 / HD))
    angles = positions[:, None] * inv_freq[None, :]
    cosine = jnp.cos(angles)[:, None, :]
    sine_part = jnp.sin(angles)[:, None, :]
    first_half = values[..., :half_dim]
    second_half = values[..., half_dim:]
    return jnp.concatenate(
        [
            first_half * cosine - second_half * sine_part,
            second_half * cosine + first_half * sine_part,
        ],
        axis=-1,
    )


GY_MASK = {"x1": 4, "x3": 12, "z1": 1, "z3": 3}
GX_MASK = {"y1": 2, "y3": 6, "core": 1}
ORDERS = (
    (("x1", "z1", "x3", "z3"), ("z3", "x3", "z1", "x1")),
    (("x3", "z3", "x1", "z1"), ("z1", "x1", "z3", "x3")),
)


def swap(value, pairing):
    if pairing in GY_MASK:
        return lax.ppermute(value, "gy", [(j, j ^ GY_MASK[pairing]) for j in range(16)])
    return lax.ppermute(value, "gx", [(g, g ^ GX_MASK[pairing]) for g in range(8)])


def add(a, b):
    return a.astype(f32) + b.astype(f32)


def scatter_gy(kept, sent, orders, both):
    got = [swap(v, orders[f][0]) for f, v in enumerate(sent)]
    flows = [add(v, g).astype(bf16) for v, g in zip(kept, got)]
    for step in (1, 2):
        half = flows[0].shape[0] // 2
        got = [swap(v[half:], orders[f][step]) for f, v in enumerate(flows)]
        flows = [add(v[:half], g).astype(bf16) for v, g in zip(flows, got)]
    half = flows[0].shape[0] // 2
    if both:
        got = [swap(v, orders[f][3]) for f, v in enumerate(flows)]
        got = [jnp.concatenate([g[half:], g[:half]], axis=0) for g in got]
        return [add(v, g) for v, g in zip(flows, got)]
    got = [swap(v[half:], orders[f][3]) for f, v in enumerate(flows)]
    return [add(v[:half], g) for v, g in zip(flows, got)]


def gather_gy(flows, orders, have):
    for step in reversed(range(4 - have)):
        got = [swap(v, orders[f][step]) for f, v in enumerate(flows)]
        flows = [jnp.concatenate([v, g], axis=0) for v, g in zip(flows, got)]
    return flows


def sum_gx(value, core):
    half = value.shape[0] // 2
    kept = lax.dynamic_slice_in_dim(value, core * half, half, 0)
    sent = lax.dynamic_slice_in_dim(value, (1 - core) * half, half, 0)
    total = kept.astype(f32) + swap(sent, "core").astype(f32)
    quarter = half // 2
    parts = [total[:quarter], total[quarter:]]
    for pairings in (("y1", "y3"), ("y3", "y1")):
        parts = [p.astype(bf16) for p in parts]
        got = [swap(p, pairing) for p, pairing in zip(parts, pairings)]
        parts = [p.astype(f32) + g.astype(f32) for p, g in zip(parts, got)]
    return jnp.concatenate(parts, axis=0)


def join_core(value, core):
    other = swap(value, "core")
    first = core == 0
    return jnp.concatenate(
        [jnp.where(first, value, other), jnp.where(first, other, value)], axis=0
    )


def project_kernel(tokens_ref, gain_ref, query_ref, keyval_ref, *outs):
    kept, sent, own = outs[:4], outs[4:8], outs[8:]
    steps, count, _ = tokens_ref.shape
    rows = count // 2
    half = rows // 2
    run = rows // 16
    query_cols = query_ref.shape[1]
    cols = query_cols + keyval_ref.shape[1]
    me, core = lax.axis_index("gy"), lax.axis_index("gx") % 2
    place = lax.broadcasted_iota(jnp.int32, (rows, 128), 0)
    lane = lax.broadcasted_iota(jnp.int32, (rows, 128), 1)
    block, inner = place // run, place % run
    gain = gain_ref[...].astype(f32).reshape(1, -1)
    for part in range(2):
        for s in range(steps):
            f = part * steps + s
            away = jnp.zeros_like(block)
            for bit, pairing in enumerate(ORDERS[part][s]):
                away = away ^ (((block >> (3 - bit)) & 1) * GY_MASK[pairing])
            token_at = (me ^ away) * (2 * run) + part * run + inner
            order = jnp.concatenate(
                [
                    jnp.where(token_at == lane + first, 1.0, 0.0).astype(bf16)
                    for first in range(0, count, 128)
                ],
                axis=1,
            )
            current = jnp.dot(order, tokens_ref[s], preferred_element_type=f32)

            @pl.when(core == s)
            def _(current=current, part=part):
                own[part][...] = current.astype(bf16)

            squares = jnp.sum(current * current, axis=1, keepdims=True)
            squares = jnp.broadcast_to(squares, (rows, 128)).astype(bf16)
            scaled = (current * gain).astype(bf16)
            query = jnp.dot(scaled, query_ref[...], preferred_element_type=f32).astype(bf16)
            keyval = jnp.dot(scaled, keyval_ref[...], preferred_element_type=f32).astype(bf16)
            for ref, at in ((kept[f], slice(0, half)), (sent[f], slice(half, rows))):
                ref[:, :query_cols] = query[at]
                ref[:, query_cols:cols] = keyval[at]
                ref[:, cols:] = squares[at]


def project(tokens, gain, query_weight, keyval_weight):
    steps, count, width = tokens.shape
    cols = query_weight.shape[1] + keyval_weight.shape[1] + 128
    rows = count // 2
    vmem = pl.BlockSpec(memory_space=pltpu.VMEM)
    flow = jax.ShapeDtypeStruct((rows // 2, cols), bf16)
    own = jax.ShapeDtypeStruct((rows, width), bf16)
    outs = pl.pallas_call(
        project_kernel,
        out_shape=[flow] * 8 + [own] * 2,
        in_specs=[vmem] * 4,
        out_specs=[vmem] * 10,
        compiler_params=pltpu.CompilerParams(vmem_limit_bytes=60 * 2**20),
        cost_estimate=pl.CostEstimate(
            flops=2 * steps * count * width * (count + cols),
            bytes_accessed=8 * 2**20,
            transcendentals=0,
        ),
    )(tokens, gain, query_weight, keyval_weight)
    return outs[:4], outs[4:8], outs[8:]


def place_kernel(own0_ref, own1_ref, other0_ref, other1_ref, out_ref):
    steps, count, _ = out_ref.shape
    rows = count // 2
    run = rows // 16
    me, core = lax.axis_index("gy"), lax.axis_index("gx") % 2
    place = lax.broadcasted_iota(jnp.int32, (8, rows), 1)
    block, inner = place // run, place % run
    token = lax.broadcasted_iota(jnp.int32, (count, rows), 0)
    for s in range(steps):
        total = None
        for part, (own, other) in enumerate(((own0_ref, other0_ref), (own1_ref, other1_ref))):
            away = jnp.zeros_like(block)
            for bit, pairing in enumerate(ORDERS[part][s]):
                away = away ^ (((block >> (3 - bit)) & 1) * GY_MASK[pairing])
            token_at = (me ^ away) * (2 * run) + part * run + inner
            order = jnp.where(token == token_at[:1], 1.0, 0.0).astype(bf16)
            value = jnp.where(core == s, own[...].astype(f32), other[...].astype(f32))
            found = jnp.dot(order, value.astype(bf16), preferred_element_type=f32)
            total = found if total is None else total + found
        out_ref[s] = total.astype(bf16)


def put_in_place(own, other):
    rows, width = own[0].shape
    vmem = pl.BlockSpec(memory_space=pltpu.VMEM)
    return pl.pallas_call(
        place_kernel,
        out_shape=jax.ShapeDtypeStruct((2, 2 * rows, width), bf16),
        in_specs=[vmem] * 4,
        out_specs=vmem,
        compiler_params=pltpu.CompilerParams(vmem_limit_bytes=16 * 2**20),
        cost_estimate=pl.CostEstimate(
            flops=16 * rows * rows * width, bytes_accessed=16 * rows * width, transcendentals=0
        ),
    )(*own, *other)


def attend(queries, cached_keys, cached_values, lengths, extra_keys, extra_values):
    scale_factor = 1.0 / math.sqrt(HD)
    cached = (
        jnp.einsum("sqd,std->sqt", queries, cached_keys, preferred_element_type=f32)
        * scale_factor
    )
    valid = jnp.arange(cached_keys.shape[1])[None, :] < lengths[:, None]
    cached = jnp.where(valid[:, None, :], cached, -1e30)
    recent = (
        jnp.sum(
            queries.astype(f32)[:, :, None, :] * extra_keys.astype(f32)[:, None, :, :], axis=-1
        )
        * scale_factor
    )
    step_of = jnp.arange(2 * GROUP) // GROUP
    seen = jnp.arange(2)[None, :] <= step_of[:, None]
    recent = jnp.where(seen[None], recent, -1e30)
    highest = jnp.maximum(
        jnp.max(cached, axis=-1, keepdims=True), jnp.max(recent, axis=-1, keepdims=True)
    )
    cached_exp = jnp.exp(cached - highest)
    recent_exp = jnp.exp(recent - highest)
    totals = jnp.sum(cached_exp, axis=-1, keepdims=True) + jnp.sum(
        recent_exp, axis=-1, keepdims=True
    )
    cached_probs = (cached_exp / totals).astype(bf16)
    recent_probs = (recent_exp / totals).astype(bf16).astype(f32)
    mixed = jnp.einsum("sqt,std->sqd", cached_probs, cached_values, preferred_element_type=f32)
    for e in range(2):
        mixed = mixed + recent_probs[:, :, e, None] * extra_values[:, e].astype(f32)[:, None, :]
    return mixed.astype(bf16)


def per_device(
    tokens,
    cache_lengths,
    key_cache,
    value_cache,
    attn_gain,
    query_weight,
    keyval_weight,
    out_weight,
    ffn_gain,
    gate_weight,
    up_weight,
    down_weight,
):
    steps, count, width = tokens.shape
    seqs = cache_lengths.shape[0]
    query_cols = query_weight.shape[1]
    hidden = gate_weight.shape[1]
    core = lax.axis_index("gx") % 2
    run = seqs // 2
    flow_rows = 16 * run
    def product(a, b):
        return jnp.dot(a, b, preferred_element_type=f32)

    def with_squares(parts, squares):
        extra = jnp.broadcast_to(squares[:, None], (squares.shape[0], 128))
        return jnp.concatenate([p.astype(bf16) for p in parts + [extra]], axis=1)

    def attention(part, summed):
        own = slice(part * run, (part + 1) * run)
        lengths = cache_lengths[own]
        queries, keys_new, values_new = [], [], []
        for s in range(steps):
            scale = lax.rsqrt(summed[s][:, query_cols + 2 * HD :][:, :1] / D + epsilon)
            projected = summed[s][:, : query_cols + 2 * HD] * scale
            rotated = rotary(
                projected[:, : query_cols + HD].reshape(run, -1, HD), (lengths + s).astype(f32)
            ).astype(bf16)
            queries.append(rotated[:, :GROUP])
            keys_new.append(rotated[:, GROUP])
            values_new.append(projected[:, query_cols + HD :].astype(bf16))
        attended = attend(
            jnp.concatenate(queries, axis=1),
            key_cache[own, :, 0],
            value_cache[own, :, 0],
            lengths,
            jnp.stack(keys_new, axis=1),
            jnp.stack(values_new, axis=1),
        )
        return [
            attended[:, s * GROUP : (s + 1) * GROUP].reshape(run, query_cols)
            for s in range(steps)
        ]

    def summed_product(part, flows, weight, have):
        gathered = gather_gy(flows, ORDERS[part], have)
        parts = jnp.concatenate([product(g, weight).astype(bf16) for g in gathered], axis=0)
        return sum_gx(parts, core)

    def feed(part, resid_own):
        resid = join_core(resid_own, core).astype(f32)
        scaled = (resid * ffn_gain.astype(f32)).astype(bf16)
        squares = jnp.sum(resid * resid, axis=1)
        packed = []
        for f in range(steps):
            rows = slice(f * flow_rows, (f + 1) * flow_rows)
            packed.append(
                with_squares(
                    [product(scaled[rows], gate_weight), product(scaled[rows], up_weight)],
                    squares[rows],
                )
            )
        return packed

    def activate(total):
        scale = lax.rsqrt(total[:, 2 * hidden :][:, :1] / D + epsilon)
        gate = total[:, :hidden] * scale
        up = total[:, hidden : 2 * hidden] * scale
        return (jax.nn.silu(gate) * up).astype(bf16)

    halves = range(2)
    kept, sent, current = project(tokens, attn_gain, query_weight, keyval_weight)
    summed = [
        scatter_gy(kept[2 * p : 2 * p + 2], sent[2 * p : 2 * p + 2], ORDERS[p], False)
        for p in halves
    ]
    mixed = [attention(p, summed[p]) for p in halves]
    outs = [summed_product(p, mixed[p], out_weight, 0) for p in halves]
    resid_own = [(current[p].astype(f32) + outs[p]).astype(bf16) for p in halves]
    packed = [feed(p, resid_own[p]) for p in halves]
    half = flow_rows // 2
    totals = [
        scatter_gy([v[:half] for v in packed[p]], [v[half:] for v in packed[p]], ORDERS[p], True)
        for p in halves
    ]
    activated = [[activate(t) for t in totals[p]] for p in halves]
    downs = [summed_product(p, activated[p], down_weight, 1) for p in halves]
    finals = [(resid_own[p].astype(f32) + downs[p]).astype(bf16) for p in halves]
    return put_in_place(finals, [swap(v, "core") for v in finals])


def solution(mesh):
    in_specs = (
        P(None, None, "gy"),
        P("gy"),
        P("gy", None, "gx", None),
        P("gy", None, "gx", None),
        P("gy"),
        P("gy", "gx"),
        P("gy", "gx"),
        P("gx", "gy"),
        P("gy"),
        P("gy", "gx"),
        P("gy", "gx"),
        P("gx", "gy"),
    )
    out_specs = P(None, None, "gy")
    return jax.shard_map(
        per_device, mesh=mesh, in_specs=in_specs, out_specs=out_specs, check_vma=False
    )
```

```python
import math

import jax
import jax.numpy as jnp
from jax import lax
from jax.experimental import pallas as pl
from jax.experimental.pallas import tpu as pltpu
from jax.sharding import PartitionSpec as P

D = 8192
HD = 128
GROUP = 8
bf16 = jnp.bfloat16
f32 = jnp.float32

epsilon = 1e-05
rotary_base = 500000.0


def rotary(values, positions):
    half_dim = HD // 2
    inv_freq = rotary_base ** (-(jnp.arange(half_dim, dtype=f32) * 2.0 / HD))
    angles = positions[:, None] * inv_freq[None, :]
    cosine = jnp.cos(angles)[:, None, :]
    sine_part = jnp.sin(angles)[:, None, :]
    first_half = values[..., :half_dim]
    second_half = values[..., half_dim:]
    return jnp.concatenate(
        [
            first_half * cosine - second_half * sine_part,
            second_half * cosine + first_half * sine_part,
        ],
        axis=-1,
    )


GY_MASK = {"x1": 4, "x3": 12, "z1": 1, "z3": 3}
GX_MASK = {"y1": 2, "y3": 6, "core": 1}
ORDERS = (
    (("x1", "z1", "x3", "z3"), ("z3", "x3", "z1", "x1")),
    (("x3", "z3", "x1", "z1"), ("z1", "x1", "z3", "x3")),
)


def swap(value, pairing):
    if pairing in GY_MASK:
        return lax.ppermute(value, "gy", [(j, j ^ GY_MASK[pairing]) for j in range(16)])
    return lax.ppermute(value, "gx", [(g, g ^ GX_MASK[pairing]) for g in range(8)])


def add(a, b):
    return a.astype(f32) + b.astype(f32)


def scatter_gy(kept, sent, orders, both):
    got = [swap(v, orders[f][0]) for f, v in enumerate(sent)]
    flows = [add(v, g).astype(bf16) for v, g in zip(kept, got)]
    for step in (1, 2):
        half = flows[0].shape[0] // 2
        got = [swap(v[half:], orders[f][step]) for f, v in enumerate(flows)]
        flows = [add(v[:half], g).astype(bf16) for v, g in zip(flows, got)]
    half = flows[0].shape[0] // 2
    if both:
        got = [swap(v, orders[f][3]) for f, v in enumerate(flows)]
        got = [jnp.concatenate([g[half:], g[:half]], axis=0) for g in got]
        return [add(v, g) for v, g in zip(flows, got)]
    got = [swap(v[half:], orders[f][3]) for f, v in enumerate(flows)]
    return [add(v[:half], g) for v, g in zip(flows, got)]


def gather_gy(flows, orders, have):
    for step in reversed(range(4 - have)):
        got = [swap(v, orders[f][step]) for f, v in enumerate(flows)]
        flows = [jnp.concatenate([v, g], axis=0) for v, g in zip(flows, got)]
    return flows


def sum_gx(value, core):
    half = value.shape[0] // 2
    kept = lax.dynamic_slice_in_dim(value, core * half, half, 0)
    sent = lax.dynamic_slice_in_dim(value, (1 - core) * half, half, 0)
    total = kept.astype(f32) + swap(sent, "core").astype(f32)
    quarter = half // 2
    parts = [total[:quarter], total[quarter:]]
    for pairings in (("y1", "y3"), ("y3", "y1")):
        parts = [p.astype(bf16) for p in parts]
        got = [swap(p, pairing) for p, pairing in zip(parts, pairings)]
        parts = [p.astype(f32) + g.astype(f32) for p, g in zip(parts, got)]
    return jnp.concatenate(parts, axis=0)


def project_kernel(tokens_ref, gain_ref, query_ref, keyval_ref, *outs):
    kept, sent, own = outs[:4], outs[4:8], outs[8:]
    steps, count, _ = tokens_ref.shape
    rows = count // 2
    half = rows // 2
    run = rows // 16
    query_cols = query_ref.shape[1]
    cols = query_cols + keyval_ref.shape[1]
    me, core = lax.axis_index("gy"), lax.axis_index("gx") % 2
    place = lax.broadcasted_iota(jnp.int32, (rows, 128), 0)
    lane = lax.broadcasted_iota(jnp.int32, (rows, 128), 1)
    block, inner = place // run, place % run
    gain = gain_ref[...].astype(f32).reshape(1, -1)
    for part in range(2):
        for s in range(steps):
            f = part * steps + s
            away = jnp.zeros_like(block)
            for bit, pairing in enumerate(ORDERS[part][s]):
                away = away ^ (((block >> (3 - bit)) & 1) * GY_MASK[pairing])
            token_at = (me ^ away) * (2 * run) + part * run + inner
            order = jnp.concatenate(
                [
                    jnp.where(token_at == lane + first, 1.0, 0.0).astype(bf16)
                    for first in range(0, count, 128)
                ],
                axis=1,
            )
            current = jnp.dot(order, tokens_ref[s], preferred_element_type=f32)

            @pl.when(core == s)
            def _(current=current, part=part):
                own[part][...] = current.astype(bf16)

            squares = jnp.sum(current * current, axis=1, keepdims=True)
            squares = jnp.broadcast_to(squares, (rows, 128)).astype(bf16)
            scaled = (current * gain).astype(bf16)
            query = jnp.dot(scaled, query_ref[...], preferred_element_type=f32).astype(bf16)
            keyval = jnp.dot(scaled, keyval_ref[...], preferred_element_type=f32).astype(bf16)
            for ref, at in ((kept[f], slice(0, half)), (sent[f], slice(half, rows))):
                ref[:, :query_cols] = query[at]
                ref[:, query_cols:cols] = keyval[at]
                ref[:, cols:] = squares[at]


def project(tokens, gain, query_weight, keyval_weight):
    steps, count, width = tokens.shape
    cols = query_weight.shape[1] + keyval_weight.shape[1] + 128
    rows = count // 2
    vmem = pl.BlockSpec(memory_space=pltpu.VMEM)
    flow = jax.ShapeDtypeStruct((rows // 2, cols), bf16)
    own = jax.ShapeDtypeStruct((rows, width), bf16)
    outs = pl.pallas_call(
        project_kernel,
        out_shape=[flow] * 8 + [own] * 2,
        in_specs=[vmem] * 4,
        out_specs=[vmem] * 10,
        compiler_params=pltpu.CompilerParams(vmem_limit_bytes=60 * 2**20),
        cost_estimate=pl.CostEstimate(
            flops=2 * steps * count * width * (count + cols),
            bytes_accessed=8 * 2**20,
            transcendentals=0,
        ),
    )(tokens, gain, query_weight, keyval_weight)
    return outs[:4], outs[4:8], outs[8:]


def place_kernel(own0_ref, own1_ref, other0_ref, other1_ref, out_ref):
    steps, count, _ = out_ref.shape
    rows = count // 2
    run = rows // 16
    me, core = lax.axis_index("gy"), lax.axis_index("gx") % 2
    place = lax.broadcasted_iota(jnp.int32, (8, rows), 1)
    block, inner = place // run, place % run
    token = lax.broadcasted_iota(jnp.int32, (count, rows), 0)
    for s in range(steps):
        total = None
        for part, (own, other) in enumerate(((own0_ref, other0_ref), (own1_ref, other1_ref))):
            away = jnp.zeros_like(block)
            for bit, pairing in enumerate(ORDERS[part][s]):
                away = away ^ (((block >> (3 - bit)) & 1) * GY_MASK[pairing])
            token_at = (me ^ away) * (2 * run) + part * run + inner
            order = jnp.where(token == token_at[:1], 1.0, 0.0).astype(bf16)
            value = jnp.where(core == s, own[...].astype(f32), other[...].astype(f32))
            found = jnp.dot(order, value.astype(bf16), preferred_element_type=f32)
            total = found if total is None else total + found
        out_ref[s] = total.astype(bf16)


def put_in_place(own, other):
    rows, width = own[0].shape
    vmem = pl.BlockSpec(memory_space=pltpu.VMEM)
    return pl.pallas_call(
        place_kernel,
        out_shape=jax.ShapeDtypeStruct((2, 2 * rows, width), bf16),
        in_specs=[vmem] * 4,
        out_specs=vmem,
        compiler_params=pltpu.CompilerParams(vmem_limit_bytes=16 * 2**20),
        cost_estimate=pl.CostEstimate(
            flops=16 * rows * rows * width, bytes_accessed=16 * rows * width, transcendentals=0
        ),
    )(*own, *other)


def attend(queries, cached_keys, cached_values, lengths, extra_keys, extra_values):
    scale_factor = 1.0 / math.sqrt(HD)
    cached = (
        jnp.einsum("sqd,std->sqt", queries, cached_keys, preferred_element_type=f32)
        * scale_factor
    )
    valid = jnp.arange(cached_keys.shape[1])[None, :] < lengths[:, None]
    cached = jnp.where(valid[:, None, :], cached, -1e30)
    recent = (
        jnp.sum(
            queries.astype(f32)[:, :, None, :] * extra_keys.astype(f32)[:, None, :, :], axis=-1
        )
        * scale_factor
    )
    step_of = jnp.arange(2 * GROUP) // GROUP
    seen = jnp.arange(2)[None, :] <= step_of[:, None]
    recent = jnp.where(seen[None], recent, -1e30)
    highest = jnp.maximum(
        jnp.max(cached, axis=-1, keepdims=True), jnp.max(recent, axis=-1, keepdims=True)
    )
    cached_exp = jnp.exp(cached - highest)
    recent_exp = jnp.exp(recent - highest)
    totals = jnp.sum(cached_exp, axis=-1, keepdims=True) + jnp.sum(
        recent_exp, axis=-1, keepdims=True
    )
    cached_probs = (cached_exp / totals).astype(bf16)
    recent_probs = (recent_exp / totals).astype(bf16).astype(f32)
    mixed = jnp.einsum("sqt,std->sqd", cached_probs, cached_values, preferred_element_type=f32)
    for e in range(2):
        mixed = mixed + recent_probs[:, :, e, None] * extra_values[:, e].astype(f32)[:, None, :]
    return mixed.astype(bf16)


def feed_kernel(own0_ref, own1_ref, other0_ref, other1_ref, gain_ref, gate_ref, up_ref, *outs):
    rows = own0_ref.shape[0]
    half = rows // 2
    hidden = gate_ref.shape[1]
    core = lax.axis_index("gx") % 2
    gain = gain_ref[...].astype(f32).reshape(1, -1)
    for part, (own, other) in enumerate(((own0_ref, other0_ref), (own1_ref, other1_ref))):
        for s in range(2):
            f = part * 2 + s
            resid = jnp.where(core == s, own[...].astype(f32), other[...].astype(f32))
            squares = jnp.sum(resid * resid, axis=1, keepdims=True)
            squares = jnp.broadcast_to(squares, (rows, 128)).astype(bf16)
            scaled = (resid * gain).astype(bf16)
            gate = jnp.dot(scaled, gate_ref[...], preferred_element_type=f32).astype(bf16)
            up = jnp.dot(scaled, up_ref[...], preferred_element_type=f32).astype(bf16)
            for ref, at in ((outs[f], slice(0, half)), (outs[4 + f], slice(half, rows))):
                ref[:, :hidden] = gate[at]
                ref[:, hidden : 2 * hidden] = up[at]
                ref[:, 2 * hidden :] = squares[at]


def feed(own, other, gain, gate_weight, up_weight):
    rows, width = own[0].shape
    hidden = gate_weight.shape[1]
    vmem = pl.BlockSpec(memory_space=pltpu.VMEM)
    flow = jax.ShapeDtypeStruct((rows // 2, 2 * hidden + 128), bf16)
    outs = pl.pallas_call(
        feed_kernel,
        out_shape=[flow] * 8,
        in_specs=[vmem] * 7,
        out_specs=[vmem] * 8,
        compiler_params=pltpu.CompilerParams(vmem_limit_bytes=32 * 2**20),
        cost_estimate=pl.CostEstimate(
            flops=16 * rows * width * hidden, bytes_accessed=12 * 2**20, transcendentals=0
        ),
    )(*own, *other, gain, gate_weight, up_weight)
    return outs[:4], outs[4:]


def per_device(
    tokens,
    cache_lengths,
    key_cache,
    value_cache,
    attn_gain,
    query_weight,
    keyval_weight,
    out_weight,
    ffn_gain,
    gate_weight,
    up_weight,
    down_weight,
):
    steps, count, width = tokens.shape
    seqs = cache_lengths.shape[0]
    query_cols = query_weight.shape[1]
    hidden = gate_weight.shape[1]
    core = lax.axis_index("gx") % 2
    run = seqs // 2
    flow_rows = 16 * run
    def product(a, b):
        return jnp.dot(a, b, preferred_element_type=f32)

    def attention(part, summed):
        own = slice(part * run, (part + 1) * run)
        lengths = cache_lengths[own]
        queries, keys_new, values_new = [], [], []
        for s in range(steps):
            scale = lax.rsqrt(summed[s][:, query_cols + 2 * HD :][:, :1] / D + epsilon)
            projected = summed[s][:, : query_cols + 2 * HD] * scale
            rotated = rotary(
                projected[:, : query_cols + HD].reshape(run, -1, HD), (lengths + s).astype(f32)
            ).astype(bf16)
            queries.append(rotated[:, :GROUP])
            keys_new.append(rotated[:, GROUP])
            values_new.append(projected[:, query_cols + HD :].astype(bf16))
        attended = attend(
            jnp.concatenate(queries, axis=1),
            key_cache[own, :, 0],
            value_cache[own, :, 0],
            lengths,
            jnp.stack(keys_new, axis=1),
            jnp.stack(values_new, axis=1),
        )
        return [
            attended[:, s * GROUP : (s + 1) * GROUP].reshape(run, query_cols)
            for s in range(steps)
        ]

    def summed_product(part, flows, weight, have):
        gathered = gather_gy(flows, ORDERS[part], have)
        parts = jnp.concatenate([product(g, weight).astype(bf16) for g in gathered], axis=0)
        return sum_gx(parts, core)

    def activate(total):
        scale = lax.rsqrt(total[:, 2 * hidden :][:, :1] / D + epsilon)
        gate = total[:, :hidden] * scale
        up = total[:, hidden : 2 * hidden] * scale
        return (jax.nn.silu(gate) * up).astype(bf16)

    halves = range(2)
    kept, sent, current = project(tokens, attn_gain, query_weight, keyval_weight)
    summed = [
        scatter_gy(kept[2 * p : 2 * p + 2], sent[2 * p : 2 * p + 2], ORDERS[p], False)
        for p in halves
    ]
    mixed = [attention(p, summed[p]) for p in halves]
    outs = [summed_product(p, mixed[p], out_weight, 0) for p in halves]
    resid_own = [(current[p].astype(f32) + outs[p]).astype(bf16) for p in halves]
    others = [swap(v, "core") for v in resid_own]
    kept, sent = feed(resid_own, others, ffn_gain, gate_weight, up_weight)
    totals = [
        scatter_gy(kept[2 * p : 2 * p + 2], sent[2 * p : 2 * p + 2], ORDERS[p], True)
        for p in halves
    ]
    activated = [[activate(t) for t in totals[p]] for p in halves]
    downs = [summed_product(p, activated[p], down_weight, 1) for p in halves]
    finals = [(resid_own[p].astype(f32) + downs[p]).astype(bf16) for p in halves]
    return put_in_place(finals, [swap(v, "core") for v in finals])


def solution(mesh):
    in_specs = (
        P(None, None, "gy"),
        P("gy"),
        P("gy", None, "gx", None),
        P("gy", None, "gx", None),
        P("gy"),
        P("gy", "gx"),
        P("gy", "gx"),
        P("gx", "gy"),
        P("gy"),
        P("gy", "gx"),
        P("gy", "gx"),
        P("gx", "gy"),
    )
    out_specs = P(None, None, "gy")
    return jax.shard_map(
        per_device, mesh=mesh, in_specs=in_specs, out_specs=out_specs, check_vma=False
    )
```

```python
import math

import jax
import jax.numpy as jnp
from jax import lax
from jax.experimental import pallas as pl
from jax.experimental.pallas import tpu as pltpu
from jax.sharding import PartitionSpec as P

D = 8192
HD = 128
GROUP = 8
bf16 = jnp.bfloat16
f32 = jnp.float32

epsilon = 1e-05
rotary_base = 500000.0


def rotary(values, positions):
    half_dim = HD // 2
    inv_freq = rotary_base ** (-(jnp.arange(half_dim, dtype=f32) * 2.0 / HD))
    angles = positions[:, None] * inv_freq[None, :]
    cosine = jnp.cos(angles)[:, None, :]
    sine_part = jnp.sin(angles)[:, None, :]
    first_half = values[..., :half_dim]
    second_half = values[..., half_dim:]
    return jnp.concatenate(
        [
            first_half * cosine - second_half * sine_part,
            second_half * cosine + first_half * sine_part,
        ],
        axis=-1,
    )


GY_MASK = {"x1": 4, "x3": 12, "z1": 1, "z3": 3}
GX_MASK = {"y1": 2, "y3": 6, "core": 1}
ORDERS = (
    (("x1", "z1", "x3", "z3"), ("z3", "x3", "z1", "x1")),
    (("x3", "z3", "x1", "z1"), ("z1", "x1", "z3", "x3")),
)


def swap(value, pairing):
    if pairing in GY_MASK:
        return lax.ppermute(value, "gy", [(j, j ^ GY_MASK[pairing]) for j in range(16)])
    return lax.ppermute(value, "gx", [(g, g ^ GX_MASK[pairing]) for g in range(8)])


def add(a, b):
    return a.astype(f32) + b.astype(f32)


def scatter_gy(kept, sent, orders, both):
    got = [swap(v, orders[f][0]) for f, v in enumerate(sent)]
    flows = [add(v, g).astype(bf16) for v, g in zip(kept, got)]
    for step in (1, 2):
        half = flows[0].shape[0] // 2
        got = [swap(v[half:], orders[f][step]) for f, v in enumerate(flows)]
        flows = [add(v[:half], g).astype(bf16) for v, g in zip(flows, got)]
    half = flows[0].shape[0] // 2
    if both:
        got = [swap(v, orders[f][3]) for f, v in enumerate(flows)]
        got = [jnp.concatenate([g[half:], g[:half]], axis=0) for g in got]
        return [add(v, g) for v, g in zip(flows, got)]
    got = [swap(v[half:], orders[f][3]) for f, v in enumerate(flows)]
    return [add(v[:half], g) for v, g in zip(flows, got)]


def gather_gy(flows, orders, have):
    for step in reversed(range(4 - have)):
        got = [swap(v, orders[f][step]) for f, v in enumerate(flows)]
        flows = [jnp.concatenate([v, g], axis=0) for v, g in zip(flows, got)]
    return flows


def sum_gx(values, core):
    half = values[0].shape[0]
    kept = jnp.where(core == 0, values[0], values[1])
    sent = jnp.where(core == 0, values[1], values[0])
    total = kept.astype(f32) + swap(sent, "core").astype(f32)
    quarter = half // 2
    parts = [total[:quarter], total[quarter:]]
    for pairings in (("y1", "y3"), ("y3", "y1")):
        parts = [p.astype(bf16) for p in parts]
        got = [swap(p, pairing) for p, pairing in zip(parts, pairings)]
        parts = [p.astype(f32) + g.astype(f32) for p, g in zip(parts, got)]
    return jnp.concatenate(parts, axis=0)


def project_kernel(tokens_ref, gain_ref, query_ref, keyval_ref, *outs):
    kept, sent, own = outs[:4], outs[4:8], outs[8:]
    steps, count, _ = tokens_ref.shape
    rows = count // 2
    half = rows // 2
    run = rows // 16
    query_cols = query_ref.shape[1]
    cols = query_cols + keyval_ref.shape[1]
    me, core = lax.axis_index("gy"), lax.axis_index("gx") % 2
    place = lax.broadcasted_iota(jnp.int32, (rows, 128), 0)
    lane = lax.broadcasted_iota(jnp.int32, (rows, 128), 1)
    block, inner = place // run, place % run
    gain = gain_ref[...].astype(f32).reshape(1, -1)
    for part in range(2):
        for s in range(steps):
            f = part * steps + s
            away = jnp.zeros_like(block)
            for bit, pairing in enumerate(ORDERS[part][s]):
                away = away ^ (((block >> (3 - bit)) & 1) * GY_MASK[pairing])
            token_at = (me ^ away) * (2 * run) + part * run + inner
            order = jnp.concatenate(
                [
                    jnp.where(token_at == lane + first, 1.0, 0.0).astype(bf16)
                    for first in range(0, count, 128)
                ],
                axis=1,
            )
            current = jnp.dot(order, tokens_ref[s], preferred_element_type=f32)

            @pl.when(core == s)
            def _(current=current, part=part):
                own[part][...] = current.astype(bf16)

            squares = jnp.sum(current * current, axis=1, keepdims=True)
            squares = jnp.broadcast_to(squares, (rows, 128)).astype(bf16)
            scaled = (current * gain).astype(bf16)
            query = jnp.dot(scaled, query_ref[...], preferred_element_type=f32).astype(bf16)
            keyval = jnp.dot(scaled, keyval_ref[...], preferred_element_type=f32).astype(bf16)
            for ref, at in ((kept[f], slice(0, half)), (sent[f], slice(half, rows))):
                ref[:, :query_cols] = query[at]
                ref[:, query_cols:cols] = keyval[at]
                ref[:, cols:] = squares[at]


def project(tokens, gain, query_weight, keyval_weight):
    steps, count, width = tokens.shape
    cols = query_weight.shape[1] + keyval_weight.shape[1] + 128
    rows = count // 2
    vmem = pl.BlockSpec(memory_space=pltpu.VMEM)
    flow = jax.ShapeDtypeStruct((rows // 2, cols), bf16)
    own = jax.ShapeDtypeStruct((rows, width), bf16)
    outs = pl.pallas_call(
        project_kernel,
        out_shape=[flow] * 8 + [own] * 2,
        in_specs=[vmem] * 4,
        out_specs=[vmem] * 10,
        compiler_params=pltpu.CompilerParams(vmem_limit_bytes=60 * 2**20),
        cost_estimate=pl.CostEstimate(
            flops=2 * steps * count * width * (count + cols),
            bytes_accessed=8 * 2**20,
            transcendentals=0,
        ),
    )(tokens, gain, query_weight, keyval_weight)
    return outs[:4], outs[4:8], outs[8:]


def place_kernel(own0_ref, own1_ref, other0_ref, other1_ref, out_ref):
    steps, count, _ = out_ref.shape
    rows = count // 2
    run = rows // 16
    me, core = lax.axis_index("gy"), lax.axis_index("gx") % 2
    place = lax.broadcasted_iota(jnp.int32, (8, rows), 1)
    block, inner = place // run, place % run
    token = lax.broadcasted_iota(jnp.int32, (count, rows), 0)
    for s in range(steps):
        total = None
        for part, (own, other) in enumerate(((own0_ref, other0_ref), (own1_ref, other1_ref))):
            away = jnp.zeros_like(block)
            for bit, pairing in enumerate(ORDERS[part][s]):
                away = away ^ (((block >> (3 - bit)) & 1) * GY_MASK[pairing])
            token_at = (me ^ away) * (2 * run) + part * run + inner
            order = jnp.where(token == token_at[:1], 1.0, 0.0).astype(bf16)
            value = jnp.where(core == s, own[...].astype(f32), other[...].astype(f32))
            found = jnp.dot(order, value.astype(bf16), preferred_element_type=f32)
            total = found if total is None else total + found
        out_ref[s] = total.astype(bf16)


def put_in_place(own, other):
    rows, width = own[0].shape
    vmem = pl.BlockSpec(memory_space=pltpu.VMEM)
    return pl.pallas_call(
        place_kernel,
        out_shape=jax.ShapeDtypeStruct((2, 2 * rows, width), bf16),
        in_specs=[vmem] * 4,
        out_specs=vmem,
        compiler_params=pltpu.CompilerParams(vmem_limit_bytes=16 * 2**20),
        cost_estimate=pl.CostEstimate(
            flops=16 * rows * rows * width, bytes_accessed=16 * rows * width, transcendentals=0
        ),
    )(*own, *other)


def attend(queries, cached_keys, cached_values, lengths, extra_keys, extra_values):
    scale_factor = 1.0 / math.sqrt(HD)
    cached = (
        jnp.einsum("sqd,std->sqt", queries, cached_keys, preferred_element_type=f32)
        * scale_factor
    )
    valid = jnp.arange(cached_keys.shape[1])[None, :] < lengths[:, None]
    cached = jnp.where(valid[:, None, :], cached, -1e30)
    recent = (
        jnp.sum(
            queries.astype(f32)[:, :, None, :] * extra_keys.astype(f32)[:, None, :, :], axis=-1
        )
        * scale_factor
    )
    step_of = jnp.arange(2 * GROUP) // GROUP
    seen = jnp.arange(2)[None, :] <= step_of[:, None]
    recent = jnp.where(seen[None], recent, -1e30)
    highest = jnp.maximum(
        jnp.max(cached, axis=-1, keepdims=True), jnp.max(recent, axis=-1, keepdims=True)
    )
    cached_exp = jnp.exp(cached - highest)
    recent_exp = jnp.exp(recent - highest)
    totals = jnp.sum(cached_exp, axis=-1, keepdims=True) + jnp.sum(
        recent_exp, axis=-1, keepdims=True
    )
    cached_probs = (cached_exp / totals).astype(bf16)
    recent_probs = (recent_exp / totals).astype(bf16).astype(f32)
    mixed = jnp.einsum("sqt,std->sqd", cached_probs, cached_values, preferred_element_type=f32)
    for e in range(2):
        mixed = mixed + recent_probs[:, :, e, None] * extra_values[:, e].astype(f32)[:, None, :]
    return mixed.astype(bf16)


def feed_kernel(own0_ref, own1_ref, other0_ref, other1_ref, gain_ref, gate_ref, up_ref, *outs):
    rows = own0_ref.shape[0]
    half = rows // 2
    hidden = gate_ref.shape[1]
    core = lax.axis_index("gx") % 2
    gain = gain_ref[...].astype(f32).reshape(1, -1)
    for part, (own, other) in enumerate(((own0_ref, other0_ref), (own1_ref, other1_ref))):
        for s in range(2):
            f = part * 2 + s
            resid = jnp.where(core == s, own[...].astype(f32), other[...].astype(f32))
            squares = jnp.sum(resid * resid, axis=1, keepdims=True)
            squares = jnp.broadcast_to(squares, (rows, 128)).astype(bf16)
            scaled = (resid * gain).astype(bf16)
            gate = jnp.dot(scaled, gate_ref[...], preferred_element_type=f32).astype(bf16)
            up = jnp.dot(scaled, up_ref[...], preferred_element_type=f32).astype(bf16)
            for ref, at in ((outs[f], slice(0, half)), (outs[4 + f], slice(half, rows))):
                ref[:, :hidden] = gate[at]
                ref[:, hidden : 2 * hidden] = up[at]
                ref[:, 2 * hidden :] = squares[at]


def feed(own, other, gain, gate_weight, up_weight):
    rows, width = own[0].shape
    hidden = gate_weight.shape[1]
    vmem = pl.BlockSpec(memory_space=pltpu.VMEM)
    flow = jax.ShapeDtypeStruct((rows // 2, 2 * hidden + 128), bf16)
    outs = pl.pallas_call(
        feed_kernel,
        out_shape=[flow] * 8,
        in_specs=[vmem] * 7,
        out_specs=[vmem] * 8,
        compiler_params=pltpu.CompilerParams(vmem_limit_bytes=32 * 2**20),
        cost_estimate=pl.CostEstimate(
            flops=16 * rows * width * hidden, bytes_accessed=12 * 2**20, transcendentals=0
        ),
    )(*own, *other, gain, gate_weight, up_weight)
    return outs[:4], outs[4:]


def per_device(
    tokens,
    cache_lengths,
    key_cache,
    value_cache,
    attn_gain,
    query_weight,
    keyval_weight,
    out_weight,
    ffn_gain,
    gate_weight,
    up_weight,
    down_weight,
):
    steps, count, width = tokens.shape
    seqs = cache_lengths.shape[0]
    query_cols = query_weight.shape[1]
    hidden = gate_weight.shape[1]
    core = lax.axis_index("gx") % 2
    run = seqs // 2
    flow_rows = 16 * run
    def product(a, b):
        return jnp.dot(a, b, preferred_element_type=f32)

    def attention(part, summed):
        own = slice(part * run, (part + 1) * run)
        lengths = cache_lengths[own]
        queries, keys_new, values_new = [], [], []
        for s in range(steps):
            scale = lax.rsqrt(summed[s][:, query_cols + 2 * HD :][:, :1] / D + epsilon)
            projected = summed[s][:, : query_cols + 2 * HD] * scale
            rotated = rotary(
                projected[:, : query_cols + HD].reshape(run, -1, HD), (lengths + s).astype(f32)
            ).astype(bf16)
            queries.append(rotated[:, :GROUP])
            keys_new.append(rotated[:, GROUP])
            values_new.append(projected[:, query_cols + HD :].astype(bf16))
        attended = attend(
            jnp.concatenate(queries, axis=1),
            key_cache[own, :, 0],
            value_cache[own, :, 0],
            lengths,
            jnp.stack(keys_new, axis=1),
            jnp.stack(values_new, axis=1),
        )
        return [
            attended[:, s * GROUP : (s + 1) * GROUP].reshape(run, query_cols)
            for s in range(steps)
        ]

    def summed_product(part, flows, weight, have):
        gathered = gather_gy(flows, ORDERS[part], have)
        return sum_gx([product(g, weight).astype(bf16) for g in gathered], core)

    def activate(total):
        scale = lax.rsqrt(total[:, 2 * hidden :][:, :1] / D + epsilon)
        gate = total[:, :hidden] * scale
        up = total[:, hidden : 2 * hidden] * scale
        return (jax.nn.silu(gate) * up).astype(bf16)

    halves = range(2)
    kept, sent, current = project(tokens, attn_gain, query_weight, keyval_weight)
    summed = [
        scatter_gy(kept[2 * p : 2 * p + 2], sent[2 * p : 2 * p + 2], ORDERS[p], False)
        for p in halves
    ]
    mixed = [attention(p, summed[p]) for p in halves]
    outs = [summed_product(p, mixed[p], out_weight, 0) for p in halves]
    resid_own = [(current[p].astype(f32) + outs[p]).astype(bf16) for p in halves]
    others = [swap(v, "core") for v in resid_own]
    kept, sent = feed(resid_own, others, ffn_gain, gate_weight, up_weight)
    totals = [
        scatter_gy(kept[2 * p : 2 * p + 2], sent[2 * p : 2 * p + 2], ORDERS[p], True)
        for p in halves
    ]
    activated = [[activate(t) for t in totals[p]] for p in halves]
    downs = [summed_product(p, activated[p], down_weight, 1) for p in halves]
    finals = [(resid_own[p].astype(f32) + downs[p]).astype(bf16) for p in halves]
    return put_in_place(finals, [swap(v, "core") for v in finals])


def solution(mesh):
    in_specs = (
        P(None, None, "gy"),
        P("gy"),
        P("gy", None, "gx", None),
        P("gy", None, "gx", None),
        P("gy"),
        P("gy", "gx"),
        P("gy", "gx"),
        P("gx", "gy"),
        P("gy"),
        P("gy", "gx"),
        P("gy", "gx"),
        P("gx", "gy"),
    )
    out_specs = P(None, None, "gy")
    return jax.shard_map(
        per_device, mesh=mesh, in_specs=in_specs, out_specs=out_specs, check_vma=False
    )
```

```python
import math

import jax
import jax.numpy as jnp
from jax import lax
from jax.experimental import pallas as pl
from jax.experimental.pallas import tpu as pltpu
from jax.sharding import PartitionSpec as P

D = 8192
HD = 128
GROUP = 8
bf16 = jnp.bfloat16
f32 = jnp.float32

epsilon = 1e-05
rotary_base = 500000.0


def rotary(values, positions):
    half_dim = HD // 2
    inv_freq = rotary_base ** (-(jnp.arange(half_dim, dtype=f32) * 2.0 / HD))
    angles = positions[:, None] * inv_freq[None, :]
    cosine = jnp.cos(angles)[:, None, :]
    sine_part = jnp.sin(angles)[:, None, :]
    first_half = values[..., :half_dim]
    second_half = values[..., half_dim:]
    return jnp.concatenate(
        [
            first_half * cosine - second_half * sine_part,
            second_half * cosine + first_half * sine_part,
        ],
        axis=-1,
    )


GY_MASK = {"x1": 4, "x3": 12, "z1": 1, "z3": 3}
GX_MASK = {"y1": 2, "y3": 6, "core": 1}
ORDERS = (
    (("x1", "z1", "x3", "z3"), ("x3", "z3", "x1", "z1")),
    (("z1", "x1", "z3", "x3"), ("z3", "x3", "z1", "x1")),
)


def swap(value, pairing):
    if pairing in GY_MASK:
        return lax.ppermute(value, "gy", [(j, j ^ GY_MASK[pairing]) for j in range(16)])
    return lax.ppermute(value, "gx", [(g, g ^ GX_MASK[pairing]) for g in range(8)])


def add(a, b):
    return a.astype(f32) + b.astype(f32)


def scatter_gy(kept, sent, orders, both):
    got = [swap(v, orders[f][0]) for f, v in enumerate(sent)]
    flows = [add(v, g).astype(bf16) for v, g in zip(kept, got)]
    for step in (1, 2):
        half = flows[0].shape[0] // 2
        got = [swap(v[half:], orders[f][step]) for f, v in enumerate(flows)]
        flows = [add(v[:half], g).astype(bf16) for v, g in zip(flows, got)]
    half = flows[0].shape[0] // 2
    if both:
        got = [swap(v, orders[f][3]) for f, v in enumerate(flows)]
        got = [jnp.concatenate([g[half:], g[:half]], axis=0) for g in got]
        return [add(v, g) for v, g in zip(flows, got)]
    got = [swap(v[half:], orders[f][3]) for f, v in enumerate(flows)]
    return [add(v[:half], g) for v, g in zip(flows, got)]


def gather_gy(flows, orders, have):
    for step in reversed(range(4 - have)):
        got = [swap(v, orders[f][step]) for f, v in enumerate(flows)]
        flows = [jnp.concatenate([v, g], axis=0) for v, g in zip(flows, got)]
    return flows


def sum_gx(values, core):
    half = values[0].shape[0]
    kept = jnp.where(core == 0, values[0], values[1])
    sent = jnp.where(core == 0, values[1], values[0])
    total = kept.astype(f32) + swap(sent, "core").astype(f32)
    quarter = half // 2
    parts = [total[:quarter], total[quarter:]]
    for pairings in (("y1", "y3"), ("y3", "y1")):
        parts = [p.astype(bf16) for p in parts]
        got = [swap(p, pairing) for p, pairing in zip(parts, pairings)]
        parts = [p.astype(f32) + g.astype(f32) for p, g in zip(parts, got)]
    return jnp.concatenate(parts, axis=0)


def project_kernel(tokens_ref, gain_ref, query_ref, keyval_ref, *outs):
    kept, sent, own = outs[:4], outs[4:8], outs[8:]
    steps, count, _ = tokens_ref.shape
    rows = count // 2
    half = rows // 2
    run = rows // 16
    query_cols = query_ref.shape[1]
    cols = query_cols + keyval_ref.shape[1]
    me, core = lax.axis_index("gy"), lax.axis_index("gx") % 2
    place = lax.broadcasted_iota(jnp.int32, (rows, 128), 0)
    lane = lax.broadcasted_iota(jnp.int32, (rows, 128), 1)
    block, inner = place // run, place % run
    gain = gain_ref[...].astype(f32).reshape(1, -1)
    for part in range(2):
        for s in range(steps):
            f = part * steps + s
            away = jnp.zeros_like(block)
            for bit, pairing in enumerate(ORDERS[part][s]):
                away = away ^ (((block >> (3 - bit)) & 1) * GY_MASK[pairing])
            token_at = (me ^ away) * (2 * run) + part * run + inner
            order = jnp.concatenate(
                [
                    jnp.where(token_at == lane + first, 1.0, 0.0).astype(bf16)
                    for first in range(0, count, 128)
                ],
                axis=1,
            )
            current = jnp.dot(order, tokens_ref[s], preferred_element_type=f32)

            @pl.when(core == s)
            def _(current=current, part=part):
                own[part][...] = current.astype(bf16)

            squares = jnp.sum(current * current, axis=1, keepdims=True)
            squares = jnp.broadcast_to(squares, (rows, 128)).astype(bf16)
            scaled = (current * gain).astype(bf16)
            query = jnp.dot(scaled, query_ref[...], preferred_element_type=f32).astype(bf16)
            keyval = jnp.dot(scaled, keyval_ref[...], preferred_element_type=f32).astype(bf16)
            for ref, at in ((kept[f], slice(0, half)), (sent[f], slice(half, rows))):
                ref[:, :query_cols] = query[at]
                ref[:, query_cols:cols] = keyval[at]
                ref[:, cols:] = squares[at]


def project(tokens, gain, query_weight, keyval_weight):
    steps, count, width = tokens.shape
    cols = query_weight.shape[1] + keyval_weight.shape[1] + 128
    rows = count // 2
    vmem = pl.BlockSpec(memory_space=pltpu.VMEM)
    flow = jax.ShapeDtypeStruct((rows // 2, cols), bf16)
    own = jax.ShapeDtypeStruct((rows, width), bf16)
    outs = pl.pallas_call(
        project_kernel,
        out_shape=[flow] * 8 + [own] * 2,
        in_specs=[vmem] * 4,
        out_specs=[vmem] * 10,
        compiler_params=pltpu.CompilerParams(vmem_limit_bytes=60 * 2**20),
        cost_estimate=pl.CostEstimate(
            flops=2 * steps * count * width * (count + cols),
            bytes_accessed=8 * 2**20,
            transcendentals=0,
        ),
    )(tokens, gain, query_weight, keyval_weight)
    return outs[:4], outs[4:8], outs[8:]


def place_kernel(own0_ref, own1_ref, other0_ref, other1_ref, out_ref):
    steps, count, _ = out_ref.shape
    rows = count // 2
    run = rows // 16
    me, core = lax.axis_index("gy"), lax.axis_index("gx") % 2
    place = lax.broadcasted_iota(jnp.int32, (8, rows), 1)
    block, inner = place // run, place % run
    token = lax.broadcasted_iota(jnp.int32, (count, rows), 0)
    for s in range(steps):
        total = None
        for part, (own, other) in enumerate(((own0_ref, other0_ref), (own1_ref, other1_ref))):
            away = jnp.zeros_like(block)
            for bit, pairing in enumerate(ORDERS[part][s]):
                away = away ^ (((block >> (3 - bit)) & 1) * GY_MASK[pairing])
            token_at = (me ^ away) * (2 * run) + part * run + inner
            order = jnp.where(token == token_at[:1], 1.0, 0.0).astype(bf16)
            value = jnp.where(core == s, own[...].astype(f32), other[...].astype(f32))
            found = jnp.dot(order, value.astype(bf16), preferred_element_type=f32)
            total = found if total is None else total + found
        out_ref[s] = total.astype(bf16)


def put_in_place(own, other):
    rows, width = own[0].shape
    vmem = pl.BlockSpec(memory_space=pltpu.VMEM)
    return pl.pallas_call(
        place_kernel,
        out_shape=jax.ShapeDtypeStruct((2, 2 * rows, width), bf16),
        in_specs=[vmem] * 4,
        out_specs=vmem,
        compiler_params=pltpu.CompilerParams(vmem_limit_bytes=16 * 2**20),
        cost_estimate=pl.CostEstimate(
            flops=16 * rows * rows * width, bytes_accessed=16 * rows * width, transcendentals=0
        ),
    )(*own, *other)


def attend(queries, cached_keys, cached_values, lengths, extra_keys, extra_values):
    scale_factor = 1.0 / math.sqrt(HD)
    cached = (
        jnp.einsum("sqd,std->sqt", queries, cached_keys, preferred_element_type=f32)
        * scale_factor
    )
    valid = jnp.arange(cached_keys.shape[1])[None, :] < lengths[:, None]
    cached = jnp.where(valid[:, None, :], cached, -1e30)
    recent = (
        jnp.sum(
            queries.astype(f32)[:, :, None, :] * extra_keys.astype(f32)[:, None, :, :], axis=-1
        )
        * scale_factor
    )
    step_of = jnp.arange(2 * GROUP) // GROUP
    seen = jnp.arange(2)[None, :] <= step_of[:, None]
    recent = jnp.where(seen[None], recent, -1e30)
    highest = jnp.maximum(
        jnp.max(cached, axis=-1, keepdims=True), jnp.max(recent, axis=-1, keepdims=True)
    )
    cached_exp = jnp.exp(cached - highest)
    recent_exp = jnp.exp(recent - highest)
    totals = jnp.sum(cached_exp, axis=-1, keepdims=True) + jnp.sum(
        recent_exp, axis=-1, keepdims=True
    )
    cached_probs = (cached_exp / totals).astype(bf16)
    recent_probs = (recent_exp / totals).astype(bf16).astype(f32)
    mixed = jnp.einsum("sqt,std->sqd", cached_probs, cached_values, preferred_element_type=f32)
    for e in range(2):
        mixed = mixed + recent_probs[:, :, e, None] * extra_values[:, e].astype(f32)[:, None, :]
    return mixed.astype(bf16)


def feed_kernel(own0_ref, own1_ref, other0_ref, other1_ref, gain_ref, gate_ref, up_ref, *outs):
    rows = own0_ref.shape[0]
    half = rows // 2
    hidden = gate_ref.shape[1]
    core = lax.axis_index("gx") % 2
    gain = gain_ref[...].astype(f32).reshape(1, -1)
    for part, (own, other) in enumerate(((own0_ref, other0_ref), (own1_ref, other1_ref))):
        for s in range(2):
            f = part * 2 + s
            resid = jnp.where(core == s, own[...].astype(f32), other[...].astype(f32))
            squares = jnp.sum(resid * resid, axis=1, keepdims=True)
            squares = jnp.broadcast_to(squares, (rows, 128)).astype(bf16)
            scaled = (resid * gain).astype(bf16)
            gate = jnp.dot(scaled, gate_ref[...], preferred_element_type=f32).astype(bf16)
            up = jnp.dot(scaled, up_ref[...], preferred_element_type=f32).astype(bf16)
            for ref, at in ((outs[f], slice(0, half)), (outs[4 + f], slice(half, rows))):
                ref[:, :hidden] = gate[at]
                ref[:, hidden : 2 * hidden] = up[at]
                ref[:, 2 * hidden :] = squares[at]


def feed(own, other, gain, gate_weight, up_weight):
    rows, width = own[0].shape
    hidden = gate_weight.shape[1]
    vmem = pl.BlockSpec(memory_space=pltpu.VMEM)
    flow = jax.ShapeDtypeStruct((rows // 2, 2 * hidden + 128), bf16)
    outs = pl.pallas_call(
        feed_kernel,
        out_shape=[flow] * 8,
        in_specs=[vmem] * 7,
        out_specs=[vmem] * 8,
        compiler_params=pltpu.CompilerParams(vmem_limit_bytes=32 * 2**20),
        cost_estimate=pl.CostEstimate(
            flops=16 * rows * width * hidden, bytes_accessed=12 * 2**20, transcendentals=0
        ),
    )(*own, *other, gain, gate_weight, up_weight)
    return outs[:4], outs[4:]


def per_device(
    tokens,
    cache_lengths,
    key_cache,
    value_cache,
    attn_gain,
    query_weight,
    keyval_weight,
    out_weight,
    ffn_gain,
    gate_weight,
    up_weight,
    down_weight,
):
    steps, count, width = tokens.shape
    seqs = cache_lengths.shape[0]
    query_cols = query_weight.shape[1]
    hidden = gate_weight.shape[1]
    core = lax.axis_index("gx") % 2
    run = seqs // 2
    flow_rows = 16 * run
    def product(a, b):
        return jnp.dot(a, b, preferred_element_type=f32)

    def attention(part, summed):
        own = slice(part * run, (part + 1) * run)
        lengths = cache_lengths[own]
        queries, keys_new, values_new = [], [], []
        for s in range(steps):
            scale = lax.rsqrt(summed[s][:, query_cols + 2 * HD :][:, :1] / D + epsilon)
            projected = summed[s][:, : query_cols + 2 * HD] * scale
            rotated = rotary(
                projected[:, : query_cols + HD].reshape(run, -1, HD), (lengths + s).astype(f32)
            ).astype(bf16)
            queries.append(rotated[:, :GROUP])
            keys_new.append(rotated[:, GROUP])
            values_new.append(projected[:, query_cols + HD :].astype(bf16))
        attended = attend(
            jnp.concatenate(queries, axis=1),
            key_cache[own, :, 0],
            value_cache[own, :, 0],
            lengths,
            jnp.stack(keys_new, axis=1),
            jnp.stack(values_new, axis=1),
        )
        return [
            attended[:, s * GROUP : (s + 1) * GROUP].reshape(run, query_cols)
            for s in range(steps)
        ]

    def summed_product(part, flows, weight, have):
        gathered = gather_gy(flows, ORDERS[part], have)
        return sum_gx([product(g, weight).astype(bf16) for g in gathered], core)

    def activate(total):
        scale = lax.rsqrt(total[:, 2 * hidden :][:, :1] / D + epsilon)
        gate = total[:, :hidden] * scale
        up = total[:, hidden : 2 * hidden] * scale
        return (jax.nn.silu(gate) * up).astype(bf16)

    halves = range(2)
    kept, sent, current = project(tokens, attn_gain, query_weight, keyval_weight)
    summed = [
        scatter_gy(kept[2 * p : 2 * p + 2], sent[2 * p : 2 * p + 2], ORDERS[p], False)
        for p in halves
    ]
    mixed = [attention(p, summed[p]) for p in halves]
    outs = [summed_product(p, mixed[p], out_weight, 0) for p in halves]
    resid_own = [(current[p].astype(f32) + outs[p]).astype(bf16) for p in halves]
    others = [swap(v, "core") for v in resid_own]
    kept, sent = feed(resid_own, others, ffn_gain, gate_weight, up_weight)
    totals = [
        scatter_gy(kept[2 * p : 2 * p + 2], sent[2 * p : 2 * p + 2], ORDERS[p], True)
        for p in halves
    ]
    activated = [[activate(t) for t in totals[p]] for p in halves]
    downs = [summed_product(p, activated[p], down_weight, 1) for p in halves]
    finals = [(resid_own[p].astype(f32) + downs[p]).astype(bf16) for p in halves]
    return put_in_place(finals, [swap(v, "core") for v in finals])


def solution(mesh):
    in_specs = (
        P(None, None, "gy"),
        P("gy"),
        P("gy", None, "gx", None),
        P("gy", None, "gx", None),
        P("gy"),
        P("gy", "gx"),
        P("gy", "gx"),
        P("gx", "gy"),
        P("gy"),
        P("gy", "gx"),
        P("gy", "gx"),
        P("gx", "gy"),
    )
    out_specs = P(None, None, "gy")
    return jax.shard_map(
        per_device, mesh=mesh, in_specs=in_specs, out_specs=out_specs, check_vma=False
    )
```
